256 devices in a mesh: sec: 64 (over z, x, core), cell: 4 (over y).
Axes of the slice: x: 4, y: 4, z: 8, core: 2. Of those that a mesh axis runs over, the one named last changes fastest.
Arguments:
- fluid_delta: float32 [7, 8, 131072], P(None, None, ('sec', 'cell')), may hold values from -6 to 6
- jacobian: bfloat16 [7, 8, 8, 131072], P(None, None, None, ('sec', 'cell')), may hold values from -0.75 to 0.75
- face_nbr: int32 [6, 131072], P(None, ('sec', 'cell')), may hold values from -128 to 128, as said below
- freq_col: float32 [7, 8, 131072], P(None, None, ('sec', 'cell')), may hold values from -6 to 6
- grid_sens: float32 [8, 3, 131072], P(None, None, ('sec', 'cell')), may hold values from -0.15625 to 0.15625
- cell_xyz: float32 [3, 131072], P(None, ('sec', 'cell')), may hold values from 0 to 1
- surf_cell: int32 [65536], P(('sec', 'cell')), may hold values from 0 to 511
- surf_owner: int32 [65536, 1], P(('sec', 'cell')), may hold values from 0 to 63; in each aligned block of 256 rows (0 to 255, 256 to 511, ...) at most 16 rows name the same one
- surf_node: int32 [65536], P(('sec', 'cell')), may hold values from 0 to 127
- load_proj: float32 [3, 8, 65536], P(None, None, ('sec', 'cell')), may hold values from -2 to 2
- surf_xyz: float32 [3, 65536], P(None, ('sec', 'cell')), may hold values from 0 to 1
- struct_delta: float32 [7, 3, 32768], P(None, None, ('sec', 'cell')), may hold values from -6 to 6
- stiffness: float32 [3, 128, 3, 32768], P(None, None, None, ('sec', 'cell')), may hold values from -0.3125 to 0.3125
- mass: float32 [3, 32768], P(None, ('sec', 'cell')), may hold values from 0.2 to 1
- omega: float32 [1], replicated, may hold values from 0.6 to 1.6
- freq_delta: float32 [1], replicated, may hold values from -4 to 4
- phase_row: float32 [7, 8, 131072], P(None, None, ('sec', 'cell')), may hold values from -0.0066439068 to 0.0066439068
Outputs:
- fluid_out: float32 [7, 8, 131072], P(None, None, ('sec', 'cell'))
- struct_out: float32 [7, 3, 32768], P(None, None, ('sec', 'cell'))
- phase_out: float32 [1], replicated
The draws below stay inside these ranges and needn't reach their ends.
Inputs may be any that keep to these rules, and one draw needn't show every extreme that they name: `face_nbr`: every nonzero offset leads to a cell of the grid; both distances 128 occur. `surf_owner`: the surface rows of one aligned block of 256 rows name one owner at most 16 times.
All inputs are finite; a program needn't handle non-finite values.
Results may differ from the reference program's by a relative error of at most 0.0003.
Values sent between devices are 32-bit elements; how exact they have to be, the bound alone decides.
No kernel may reach another device: no remote copies, remote signals or barrier semaphores. Data moves between devices by JAX's collectives and lax.ppermute only.
A program may use at most 128 MiB of HBM per device.

```python
import math
import jax
import jax.numpy as jnp
import numpy as np
from jax import lax

NT = 7
NV = 8
NF = 6
RIM = 128
C_DEV = 512
S_DEV = 256
NODE_DEV = 128
CAP = 16
CELLS = 131072
SURF = 65536
NODES = 32768
N_SEC = 64
N_CELL = 4


def draw_face_nbr(key, part):
    cell_ids = jnp.arange(CELLS, dtype=jnp.int32)
    offsets = jax.random.randint(key, (NF, CELLS), -RIM, RIM + 1).astype(jnp.int32)
    offsets = jnp.where(offsets == 0, 1, offsets)
    local_pos = cell_ids % C_DEV
    offsets = offsets.at[0].set(jnp.where(local_pos == 0, -RIM, offsets[0]))
    offsets = offsets.at[1].set(jnp.where(local_pos == C_DEV - 1, RIM, offsets[1]))
    offsets = offsets.at[2].set(jnp.ones((CELLS,), jnp.int32))
    targets = cell_ids[None, :] + offsets
    return jnp.where((targets < 0) | (targets >= CELLS), 0, offsets).astype(jnp.int32)


def draw_phase_row(key, part):
    growth = 1.0 + 2.0 * jnp.arange(CELLS, dtype=jnp.float32) / CELLS
    spread = growth / math.sqrt(NT * NV * CELLS)
    samples = jnp.clip(jax.random.normal(key, (NT, NV, CELLS), jnp.float32), -6.0, 6.0)
    return (samples * spread[None, None, :]).astype(jnp.float32)


def touch_ends(values, stream_key, low, largest):
    index_at = [jax.random.randint(jax.random.fold_in(stream_key, axis), (), 0, length) for axis, length in enumerate(values.shape)]
    longest = values.shape.index(max(values.shape))
    neighbour = index_at[:longest] + [(index_at[longest] + 1) % values.shape[longest]] + index_at[longest + 1:]
    return values.at[tuple(index_at)].set(low).at[tuple(neighbour)].set(largest)


def steps_of(own_key, dims, shards, low, high):
    def one(axis_at, parts):
        draws = jax.random.uniform(jax.random.fold_in(jax.random.fold_in(own_key, 6), axis_at), (parts,), jnp.float32, low / len(shards), high / len(shards))
        return jnp.repeat(jnp.exp(draws), dims[axis_at] // parts).reshape((-1,) + (1,) * (len(dims) - axis_at - 1))

    level = one(*shards[0])
    for cut in shards[1:]:
        level = level * one(*cut)
    return level


def shared_out(own_key, own, number, rows, count, top, most, skew):
    order = jax.random.permutation(own_key, count)
    packed, usual = load_shares(count, rows * top, most, skew, True), load_shares(count, rows * top, most, skew, False)
    places = jnp.arange(count)

    def named(sizes, offset_by):
        used = int((sizes > 0).sum())
        fixed = max(1, used // 4)
        passed = fixed + (places - fixed + offset_by * (used - fixed)) % max(1, count - fixed)
        return jnp.zeros((count,), jnp.int32).at[order[jnp.where(places < fixed, places, passed)]].set(jnp.asarray(sizes, jnp.int32))

    sizes = jnp.where(number % 4 == 0, named(packed, number // 4), named(usual, number - number // 4 - 1))
    mixed = jax.random.permutation(jax.random.fold_in(own, 3), count)
    donor, receiver = mixed[0:count // 2 * 2:2], mixed[1:count // 2 * 2:2]
    room = jnp.minimum(sizes[donor] - 1, most - sizes[receiver]) // 2
    room = jnp.where((donor == order[0]) | (receiver == order[0]) | (sizes[receiver] == 0), 0, jnp.maximum(room, 0))
    passed = jax.random.randint(jax.random.fold_in(own, 4), (count // 2,), 0, 1 << 20) % (room + 1)
    sizes = sizes.at[donor].add(-passed).at[receiver].add(passed)
    labels = jnp.searchsorted(jnp.cumsum(sizes), jnp.arange(rows * top), side="right").astype(jnp.int32)
    listing = labels.reshape(top, rows).T
    listing = listing[jax.random.permutation(jax.random.fold_in(own, 1), rows)]
    offset_by = jax.random.randint(jax.random.fold_in(own, 2), (rows, 1), 0, top)
    return jnp.take_along_axis(listing, (jnp.arange(top)[None, :] + offset_by) % top, axis=1)


def load_shares(count, total, limit, slope, full):
    portions = [(1 << 20) // math.isqrt(standing ** slope) + 1 for standing in range(1, count + 1)]
    largest = limit if full else min(limit, max(-(-total // count), total * portions[0] // sum(portions)))
    least = 1 if total - largest >= count - 1 else 0
    given, surplus = [largest] + [least] * (count - 1), total - largest - least * (count - 1)
    while surplus > 0:
        free = [i for i in range(1, count) if given[i] < largest] or [i for i in range(1, count) if given[i] < limit]
        whole, remaining = sum([portions[i] for i in free]), surplus
        for i in free:
            addition = min(limit - given[i], max(1, remaining * portions[i] // whole), surplus)
            given[i] = given[i] + addition
            surplus = surplus - addition
    return np.array(given)


def centred(rng, shape, width, most, pieces=(), kind=jnp.bfloat16):
    values = jax.random.normal(rng, shape, jnp.float32) * width
    if len(pieces) > 0:
        values = steps_of(rng, shape, pieces, -0.22, 0.18) * values
    return jnp.clip(values, min=-most, max=most).astype(kind)


def setup_inputs(seed: int = 0) -> dict:
    keys = jax.random.split(jax.random.key(seed), 18)
    fluid_delta = centred(keys[0], (NT, NV, CELLS), 1.0, 6.0, ((2, 256),), jnp.float32)
    jacobian = centred(keys[1], (NF + 1, NV, NV, CELLS), (7 * NV) ** -0.5, 0.75, ((3, 256),))
    face_nbr = draw_face_nbr(jax.random.fold_in(keys[17], 71), 0)
    freq_col = centred(keys[3], (NT, NV, CELLS), 1.0, 6.0, ((2, 256),), jnp.float32)
    grid_sens = centred(keys[4], (NV, 3, CELLS), (6 * S_DEV) ** -0.5, 0.15625, ((2, 256),), jnp.float32)
    cell_xyz = jnp.clip(1.0 * jax.random.uniform(keys[5], (3, CELLS), jnp.float32) ** steps_of(keys[5], (3, CELLS), ((1, 256),), -0.2, 0.2), 0.0, 1.0)
    surf_cell = touch_ends(jax.random.randint(keys[6], (SURF,), 0, C_DEV), jax.random.fold_in(keys[6], 1), 0, C_DEV - 1).astype(jnp.int32)
    surf_owner_keys = jax.random.split(jax.random.fold_in(keys[7], 1), SURF // S_DEV)
    surf_owner_turns = jax.random.permutation(jax.random.fold_in(keys[7], 3), SURF // S_DEV)
    surf_owner = jax.vmap(lambda own, number: shared_out(jax.random.fold_in(keys[7], 2), own, number, S_DEV, N_SEC, 1, CAP, 2))(surf_owner_keys, surf_owner_turns).reshape((SURF, 1))
    surf_node = touch_ends(jax.random.randint(keys[8], (SURF,), 0, NODE_DEV), jax.random.fold_in(keys[8], 1), 0, NODE_DEV - 1).astype(jnp.int32)
    load_proj = centred(keys[9], (3, NV, SURF), NV ** -0.5, 2.0, ((2, 256),), jnp.float32)
    surf_xyz = jnp.clip(1.0 * jax.random.uniform(keys[10], (3, SURF), jnp.float32) ** steps_of(keys[10], (3, SURF), ((1, 256),), -0.2, 0.2), 0.0, 1.0)
    struct_delta = centred(keys[11], (NT, 3, NODES), 1.0, 6.0, ((2, 256),), jnp.float32)
    stiffness = centred(keys[12], (3, NODE_DEV, 3, NODES), (3 * NODE_DEV) ** -0.5, 0.3125, ((3, 256),), jnp.float32)
    mass = jnp.clip(jnp.exp(math.log(1.0) - 1.609438 * jax.random.uniform(keys[13], (3, NODES), jnp.float32) ** steps_of(keys[13], (3, NODES), ((1, 256),), -0.2, 0.2)), 0.2, 1.0)
    omega = jnp.clip(jax.random.uniform(keys[14], (1,), jnp.float32, 0.6, 1.6), 0.6, 1.6)
    freq_delta = centred(keys[15], (1,), 1.0, 4.0, (), jnp.float32)
    phase_row = draw_phase_row(jax.random.fold_in(keys[17], 71), 0)
    return dict(fluid_delta=fluid_delta, jacobian=jacobian, face_nbr=face_nbr, freq_col=freq_col, grid_sens=grid_sens, cell_xyz=cell_xyz, surf_cell=surf_cell, surf_owner=surf_owner, surf_node=surf_node, load_proj=load_proj, surf_xyz=surf_xyz, struct_delta=struct_delta, stiffness=stiffness, mass=mass, omega=omega, freq_delta=freq_delta, phase_row=phase_row)


support_radius = 1.0

def spectral_table(instances):
    positions = np.arange(instances)
    offset = positions[:, None] - positions[None, :]
    clipped = np.where(offset == 0, 1, offset)
    values = np.where(offset == 0, 0.0, 0.5 * (-1.0) ** offset / np.sin(np.pi * clipped / instances))
    return values

def wendland(rows_xyz, cells_xyz):
    squared = (rows_xyz[0][:, None] - cells_xyz[0][None, :]) ** 2
    squared = squared + (rows_xyz[1][:, None] - cells_xyz[1][None, :]) ** 2
    squared = squared + (rows_xyz[2][:, None] - cells_xyz[2][None, :]) ** 2
    reach = jnp.sqrt(squared) / support_radius
    falloff = jnp.maximum(1.0 - reach, 0.0)
    return falloff ** 4 * (4.0 * reach + 1.0)

def reference(fluid_delta, jacobian, face_nbr, freq_col, grid_sens, cell_xyz, surf_cell, surf_owner, surf_node, load_proj, surf_xyz, struct_delta, stiffness, mass, omega, freq_delta, phase_row):
    highest = lax.Precision.HIGHEST
    table_np = spectral_table(NT)
    spectral = jnp.asarray(table_np, jnp.float32)
    second = jnp.asarray(table_np @ table_np, jnp.float32)
    cell_ids = jnp.arange(CELLS, dtype=jnp.int32)
    result = jnp.einsum('vwc,twc->tvc', jacobian[0].astype(jnp.float32), fluid_delta, precision=highest)
    for face_id in range(NF):
        step_to = face_nbr[face_id]
        present = (step_to != 0).astype(jnp.float32)
        clipped = jnp.where(step_to != 0, cell_ids + step_to, 0).astype(jnp.int32)
        values = jnp.take(fluid_delta, clipped, axis=2) * present[None, None, :]
        result = result + jnp.einsum('vwc,twc->tvc', jacobian[face_id + 1].astype(jnp.float32), values, precision=highest)
    result = result + omega[0] * jnp.einsum('ts,svc->tvc', spectral, fluid_delta, precision=highest)
    result = result + freq_delta[0] * freq_col
    devices = N_SEC * N_CELL
    row_block = (jnp.arange(SURF, dtype=jnp.int32) // S_DEV).astype(jnp.int32)
    row_column = row_block % N_CELL
    row_cellid = (row_block * C_DEV + surf_cell).astype(jnp.int32)
    row_nodeid = ((surf_owner[:, 0] * N_CELL + row_column) * NODE_DEV + surf_node).astype(jnp.int32)
    surf_values = jnp.take(fluid_delta, row_cellid, axis=2)
    row_load = jnp.einsum('kvr,tvr->tkr', load_proj, surf_values, precision=highest)
    node_load = jax.ops.segment_sum(row_load.reshape(NT * 3, SURF).T, row_nodeid, num_segments=NODES).T.reshape(NT, 3, NODES)
    stiff_block = stiffness.reshape(3, NODE_DEV, 3, devices, NODE_DEV)
    delta_block = struct_delta.reshape(NT, 3, devices, NODE_DEV)
    struct_out = jnp.einsum('kiqdj,tqdj->tkdi', stiff_block, delta_block, precision=highest).reshape(NT, 3, NODES)
    inertia = jnp.einsum('ts,skn->tkn', second, struct_delta, precision=highest)
    struct_out = struct_out + omega[0] * omega[0] * mass[None] * inertia - node_load
    surf_disp = jnp.take(struct_delta, row_nodeid, axis=2).reshape(NT * 3, SURF)
    part_rows = N_CELL * S_DEV
    part_cells = N_CELL * C_DEV
    disp_parts = surf_disp.reshape(NT * 3, N_SEC, part_rows).transpose(1, 0, 2)
    centre_parts = surf_xyz.reshape(3, N_SEC, part_rows).transpose(1, 0, 2)
    cell_parts = cell_xyz.reshape(3, N_SEC, part_cells).transpose(1, 0, 2)

    def one_part(operand):
        shifts, centres, places = operand
        return jnp.dot(shifts, wendland(centres, places), precision=highest)
    moved = lax.map(one_part, (disp_parts, centre_parts, cell_parts))
    mesh_disp = moved.transpose(1, 0, 2).reshape(NT, 3, CELLS)
    result = result + jnp.einsum('vkc,tkc->tvc', grid_sens, mesh_disp, precision=highest)
    phase_out = jnp.sum(phase_row * fluid_delta).reshape(1)
    return (result, struct_out, phase_out)
```

```python
import functools

import jax
import jax.numpy as jnp
import numpy as np
from jax import lax
from jax.experimental import pallas as pl
from jax.experimental.pallas import tpu as pltpu
from jax.sharding import PartitionSpec as P

NT = 7
NV = 8
NF = 6
L = 128
CHIPS = 32
CAP = 16
ROWS = 27
F32 = jnp.float32
BF16 = jnp.bfloat16


def spectral_table(instances):
    positions = np.arange(instances)
    offset = positions[:, None] - positions[None, :]
    clipped = np.where(offset == 0, 1, offset)
    return np.where(
        offset == 0, 0.0, 0.5 * (-1.0) ** offset / np.sin(np.pi * clipped / instances)
    )


SPECTRAL = np.asarray(spectral_table(NT), np.float32)
SECOND = np.asarray(spectral_table(NT) @ spectral_table(NT), np.float32)


def iota(shape, axis):
    return lax.broadcasted_iota(jnp.int32, shape, axis)


def lanes_of(values, index):
    return jnp.take_along_axis(values, index, axis=1, mode="promise_in_bounds")


def thirds(values):
    high = values.astype(BF16)
    rest = values - high.astype(F32)
    middle = rest.astype(BF16)
    low = (rest - middle.astype(F32)).astype(BF16)
    return jnp.concatenate([high, middle, low], axis=0)


def dot_nt(a, b, precision=None):
    return lax.dot_general(
        a, b, (((1,), (1,)), ((), ())), precision=precision, preferred_element_type=F32
    )


def prep_kernel(fluid, phase, cell, owner, node, proj, struct, out, pay):
    pay[...] = jnp.zeros_like(pay)
    for h in range(2):
        span = pl.ds(h * L, L)
        index = jnp.broadcast_to(cell[:, span], (8, L))
        lane, chunk = index & (L - 1), index >> 7
        for t in range(NT):
            got = lanes_of(fluid[t, :, pl.ds(0, L)], lane)
            for c in range(1, 4):
                got = jnp.where(chunk == c, lanes_of(fluid[t, :, pl.ds(c * L, L)], lane), got)
            for k in range(3):
                f = k * NT + t
                row = f // 6 * 8 + f % 6
                pay[pl.ds(row, 1), span] = jnp.sum(proj[k, :, span] * got, axis=0, keepdims=True)
    pay[pl.ds(27, 1), :] = (node[...] + 1).astype(F32)
    own = owner[...]
    hot = jnp.where(iota((64, 256), 0) == own, 1.0, 0.0)
    before = jnp.where(iota((256, 256), 0) < iota((256, 256), 1), 1.0, 0.0).astype(BF16)
    counts = jnp.dot(hot.astype(BF16), before, preferred_element_type=F32)
    rank = jnp.sum(hot * counts, axis=0, keepdims=True)
    slot = own * CAP + rank.astype(jnp.int32)
    slot_hot = jnp.where(iota((1024, 256), 0) == slot, 1.0, 0.0).astype(BF16)
    slotted = dot_nt(thirds(pay[...]), slot_hot)
    slotted = slotted[0:32] + slotted[32:64] + slotted[64:96]

    part = phase[0] * fluid[0]
    for t in range(1, NT):
        part = part + phase[t] * fluid[t]
    part = jnp.sum(part, axis=0, keepdims=True)
    part = part[:, 0:L] + part[:, L : 2 * L] + part[:, 2 * L : 3 * L] + part[:, 3 * L : 4 * L]
    part = part + pltpu.roll(part, 64, 1)
    part = part + pltpu.roll(part, 32, 1)
    is_phase = iota((8, L), 0) == 4
    place = iota((8, L), 1) >> 5
    for c in range(8):
        groups = [slotted[g * 8 : g * 8 + 8, c * L : c * L + L] for g in range(4)]
        groups[3] = jnp.where(is_phase, part, groups[3])
        turned = []
        for d in range(4):
            mixed = groups[d]
            for j in range(1, 4):
                mixed = jnp.where(place == j, groups[(j + d) % 4], mixed)
            turned.append(pltpu.roll(mixed, 32 * d, 1) if d else mixed)
        for j in range(4):
            packed = turned[(0 - j) % 4]
            for g in range(1, 4):
                packed = jnp.where(place == g, turned[(g - j) % 4], packed)
            base = (c * 4 + j) * ROWS
            for k in range(3):
                out[pl.ds(base + k * NT, NT), :] = struct[k]
            out[pl.ds(base + 21, 6), :] = packed[0:6]


def window_kernel(
    fluid, before, after, jac, nbr, freq, struct, stiff, mass, scal, flux, part, gathered
):
    omega, dfreq = scal[0], scal[1]
    for i in range(4):
        span = pl.ds(i * L, L)
        for f in range(NF):
            off = jnp.broadcast_to(nbr[pl.ds(f, 1), span], (8, L))
            place = iota((8, L), 1) + L + off
            lane = place & (L - 1)
            which = jnp.where(off == 0, 3, place >> 7)
            for t in range(NT):
                got = jnp.zeros((8, L), F32)
                for q in range(3):
                    j = i + q
                    if j == 0:
                        src = before[t]
                    elif j == 5:
                        src = after[t]
                    else:
                        src = fluid[t, :, pl.ds((j - 1) * L, L)]
                    got = jnp.where(which == q, lanes_of(src, lane), got)
                gathered[f, t] = got
        low_half = [(iota((8, L), 0) & s) == 0 for s in (4, 2, 1)]
        for t in range(NT):
            here = fluid[t, :, span]
            sums = [None] * 8
            for f in range(NF + 1):
                val = here if f == 0 else gathered[f - 1, t]
                for vv in range(4):
                    pair = jac[f, pl.ds(vv * 16, 16), span].astype(F32)
                    for u in range(2):
                        term = pair[u * 8 : u * 8 + 8] * val
                        v = vv * 2 + u
                        sums[v] = term if sums[v] is None else sums[v] + term
            level = sums
            for s, low in zip((4, 2, 1), low_half):
                half = len(level) // 2
                level = [
                    jnp.where(
                        low,
                        level[v] + pltpu.roll(level[v], 8 - s, 0),
                        level[v + half] + pltpu.roll(level[v + half], s, 0),
                    )
                    for v in range(half)
                ]
            total = level[0]
            turn = None
            for s in range(NT):
                if s != t:
                    term = float(SPECTRAL[t, s]) * fluid[s, :, span]
                    turn = term if turn is None else turn + term
            flux[t, :, span] = total + omega * turn + dfreq * freq[t, :, span]
    for k in range(3):
        acc = None
        for q in range(3):
            term = dot_nt(struct[q], stiff[k, q], lax.Precision.HIGHEST)
            acc = term if acc is None else acc + term
        for t in range(NT):
            turn = None
            for s in range(NT):
                term = float(SECOND[t, s]) * struct[k, pl.ds(s, 1), :]
                turn = term if turn is None else turn + term
            part[k, pl.ds(t, 1), :] = acc[t : t + 1] + omega * omega * mass[pl.ds(k, 1), :] * turn


def lookup_kernel(mine, other, owner, node, xyz, core, out):
    q = core[0]
    for h in range(2):
        span = pl.ds(h * L, L)
        own = jnp.broadcast_to(owner[:, span], (8, L))
        lane = jnp.broadcast_to(node[:, span], (8, L))
        chip = own >> 1
        same = (own & 1) == q
        found = [jnp.zeros((8, L), F32) for _ in range(3)]
        for table, key in (
            (mine, jnp.where(same, chip, -1)),
            (other, jnp.where(same, -1, chip)),
        ):
            for p in range(CHIPS):
                hit = key == p
                for k in range(3):
                    values = table[pl.ds(p * ROWS + k * NT, 8), :]
                    found[k] = jnp.where(hit, lanes_of(values, lane), found[k])
        last = iota((8, L), 0) == 7
        for k in range(3):
            centre = jnp.broadcast_to(xyz[pl.ds(k, 1), span], (8, L))
            out[pl.ds(k * 8, 8), span] = jnp.where(last, centre, found[k])
    sums = []
    for table in (mine, other):
        acc = table[pl.ds(25, 1), :]
        for p in range(1, CHIPS):
            acc = acc + table[pl.ds(p * ROWS + 25, 1), :]
        sums.append(acc)
    total = jnp.broadcast_to(sums[0] + sums[1], (8, L))
    out[pl.ds(24, 8), pl.ds(0, L)] = total
    out[pl.ds(24, 8), pl.ds(L, L)] = total


def loads_kernel(mine, other, part, core, out, dense):
    q = core[0]
    block = iota((8, L), 1) >> 4
    for a, table in enumerate((mine, other)):
        for c in range(4):
            shifted = []
            for i in range(8):
                values = table[pl.ds((c * 8 + i) * ROWS + 19, 8), :]
                shifted.append(jnp.where(q == 1, pltpu.roll(values, L - 16, 1), values))
            for g in range(4):
                packed = None
                for i in range(8):
                    turn = (16 * i - 32 * g) % L
                    moved = pltpu.roll(shifted[i], turn, 1) if turn else shifted[i]
                    packed = moved if packed is None else jnp.where(block == i, moved, packed)
                dense[pl.ds(g * 8, 8), pl.ds((a * 4 + c) * L, L)] = packed
    tags = dense[pl.ds(29, 1), :].astype(jnp.int32)
    node_hot = jnp.where(iota((L, 1024), 0) + 1 == tags, 1.0, 0.0).astype(BF16)
    loads = dot_nt(thirds(dense[...]), node_hot)
    loads = loads[0:32] + loads[32:64] + loads[64:96]
    for k in range(3):
        for t in range(NT):
            f = k * NT + t
            row = f // 6 * 8 + f % 6 + 2
            out[k, pl.ds(t, 1), :] = part[k, pl.ds(t, 1), :] - loads[row : row + 1]


def final_kernel(d0, d1, d2, d3, cells, sens, flux, out, phase_out):
    cols = jnp.concatenate([cells[...], jnp.zeros((5, 512), F32)], axis=0).T
    moved = None
    for ref in (d0, d1, d2, d3):
        squared = None
        for k in range(3):
            gap = cols[:, k : k + 1] - ref[pl.ds(k * 8 + 7, 1), :]
            squared = gap * gap if squared is None else squared + gap * gap
        dist = jnp.sqrt(squared)
        fall = jnp.maximum(1.0 - dist, 0.0)
        fall = fall * fall
        basis = fall * fall * (4.0 * dist + 1.0)
        high = basis.astype(BF16)
        low = (basis - high.astype(F32)).astype(BF16)
        shift = ref[pl.ds(0, 24), :]
        s_high = shift.astype(BF16)
        s_low = (shift - s_high.astype(F32)).astype(BF16)
        both = dot_nt(jnp.concatenate([s_high, s_low], axis=0), high)
        term = both[0:24] + both[24:48] + dot_nt(s_high, low)
        moved = term if moved is None else moved + term
    for t in range(NT):
        total = flux[t]
        for k in range(3):
            total = total + sens[k] * moved[k * 8 + t : k * 8 + t + 1]
        out[t] = total
    row = pl.ds(24, 1), pl.ds(0, L)
    total = (d0[row] + d2[row]) + (d1[row] + d3[row])
    total = jnp.where(iota((1, L), 1) >= 96, total, 0.0)
    phase_out[0, 0] = jnp.sum(total)


VM = pl.BlockSpec(memory_space=pltpu.VMEM)
SM = pl.BlockSpec(memory_space=pltpu.SMEM)


def kernel(body, name, ins, shapes, outs=None, scratch=(), flops=1000, size=100000):
    return pl.pallas_call(
        body,
        out_shape=[jax.ShapeDtypeStruct(s, F32) for s in shapes],
        in_specs=ins,
        out_specs=outs or [VM] * len(shapes),
        scratch_shapes=list(scratch),
        name=name,
        compiler_params=pltpu.CompilerParams(vmem_limit_bytes=32 * 1024 * 1024),
        cost_estimate=pl.CostEstimate(flops=flops, bytes_accessed=size, transcendentals=0),
    )


def on_device(
    fluid_delta,
    jacobian,
    face_nbr,
    freq_col,
    grid_sens,
    cell_xyz,
    surf_cell,
    surf_owner,
    surf_node,
    load_proj,
    surf_xyz,
    struct_delta,
    stiffness,
    mass,
    omega,
    freq_delta,
    phase_row,
):
    sections = lax.axis_size("sec")
    columns = lax.axis_size("cell")
    both = sections * columns
    struct = jnp.transpose(struct_delta, (1, 0, 2))
    stiff = jnp.transpose(stiffness, (0, 2, 1, 3))
    sens = jnp.transpose(grid_sens, (1, 0, 2))
    owner = surf_owner.reshape(1, 256)
    node = surf_node.reshape(1, 256)
    cell = surf_cell.reshape(1, 256)
    core = (lax.axis_index("sec") % 2).astype(jnp.int32).reshape(1)
    scal = jnp.concatenate([omega, freq_delta])

    (message,) = kernel(
        prep_kernel, "prep", [VM] * 7, [(CHIPS * ROWS, L)], scratch=[pltpu.VMEM((32, 256), F32)]
    )(fluid_delta, phase_row, cell, owner, node, load_proj, struct)
    groups = [[2 * i + c for i in range(sections // 2)] for c in range(2)]
    mine = lax.all_to_all(
        message.reshape(CHIPS, 1, ROWS * L), "sec", 0, 0, axis_index_groups=groups, tiled=True
    ).reshape(CHIPS * ROWS, L)
    up = [(i, i + 1) for i in range(both - 1)]
    down = [(i + 1, i) for i in range(both - 1)]
    before = lax.ppermute(fluid_delta[:, :, 3 * L :], ("sec", "cell"), up)
    after = lax.ppermute(fluid_delta[:, :, :L], ("sec", "cell"), down)
    flux, part = kernel(
        window_kernel,
        "window",
        [VM] * 9 + [SM],
        [(NT, NV, 512), (3, NT, L)],
        scratch=[pltpu.VMEM((NF, NT, 8, L), F32)],
        flops=10**9,
        size=4 * 10**6,
    )(
        fluid_delta,
        before,
        after,
        jacobian.reshape(NF + 1, 64, 512),
        face_nbr,
        freq_col,
        struct,
        stiff,
        mass,
        scal,
    )
    other = lax.ppermute(mine, "sec", [(i, i ^ 1) for i in range(sections)])
    (disp,) = kernel(lookup_kernel, "lookup", [VM] * 5 + [SM], [(32, 256)])(
        mine, other, owner, node, surf_xyz, core
    )
    d1, d3, d2 = (
        lax.ppermute(disp, "cell", [(i, (i + k) % columns) for i in range(columns)])
        for k in (1, 3, 2)
    )
    (struct_out,) = kernel(
        loads_kernel,
        "loads",
        [VM] * 3 + [SM],
        [(3, NT, L)],
        scratch=[pltpu.VMEM((32, 1024), F32)],
        size=2 * 10**6,
    )(mine, other, part, core)
    fluid_out, phase_out = kernel(
        final_kernel, "final", [VM] * 7, [(NT, NV, 512), (1, 1)], outs=[VM, SM]
    )(disp, d1, d2, d3, cell_xyz, sens, flux)
    return fluid_out, jnp.transpose(struct_out, (1, 0, 2)), phase_out.reshape(1)


def solution(mesh):
    split = ("sec", "cell")
    return jax.shard_map(
        on_device,
        mesh=mesh,
        in_specs=(
            P(None, None, split),
            P(None, None, None, split),
            P(None, split),
            P(None, None, split),
            P(None, None, split),
            P(None, split),
            P(split),
            P(split, None),
            P(split),
            P(None, None, split),
            P(None, split),
            P(None, None, split),
            P(None, None, None, split),
            P(None, split),
            P(),
            P(),
            P(None, None, split),
        ),
        out_specs=(P(None, None, split), P(None, None, split), P()),
        check_vma=False,
    )
```

```python
import functools

import jax
import jax.numpy as jnp
import numpy as np
from jax import lax
from jax.experimental import pallas as pl
from jax.experimental.pallas import tpu as pltpu
from jax.sharding import PartitionSpec as P

NT = 7
NV = 8
NF = 6
L = 128
CHIPS = 32
CAP = 16
ROWS = 27
F32 = jnp.float32
BF16 = jnp.bfloat16


def spectral_table(instances):
    positions = np.arange(instances)
    offset = positions[:, None] - positions[None, :]
    clipped = np.where(offset == 0, 1, offset)
    return np.where(
        offset == 0, 0.0, 0.5 * (-1.0) ** offset / np.sin(np.pi * clipped / instances)
    )


SPECTRAL = np.asarray(spectral_table(NT), np.float32)
SECOND = np.asarray(spectral_table(NT) @ spectral_table(NT), np.float32)


def iota(shape, axis):
    return lax.broadcasted_iota(jnp.int32, shape, axis)


def lanes_of(values, index):
    return jnp.take_along_axis(values, index, axis=1, mode="promise_in_bounds")


def thirds(values):
    high = values.astype(BF16)
    rest = values - high.astype(F32)
    middle = rest.astype(BF16)
    low = (rest - middle.astype(F32)).astype(BF16)
    return jnp.concatenate([high, middle, low], axis=0)


def dot_nt(a, b, precision=None):
    return lax.dot_general(
        a, b, (((1,), (1,)), ((), ())), precision=precision, preferred_element_type=F32
    )


def prep_kernel(*refs):
    far, out, pay, near, sems = refs[:7], refs[7], refs[8], refs[9:16], refs[16]
    fluid, phase, cell, owner, node, proj, struct = near
    copies = [pltpu.make_async_copy(a, b, sems.at[i]) for i, (a, b) in enumerate(zip(far, near))]
    for i in (2, 3, 4, 0, 5, 1, 6):
        copies[i].start()
    pay[...] = jnp.zeros_like(pay)
    for i in (2, 3, 4, 0, 5, 1, 6):
        copies[i].wait()
    for h in range(2):
        span = pl.ds(h * L, L)
        index = jnp.broadcast_to(cell[:, span], (8, L))
        lane, chunk = index & (L - 1), index >> 7
        for t in range(NT):
            got = lanes_of(fluid[t, :, pl.ds(0, L)], lane)
            for c in range(1, 4):
                got = jnp.where(chunk == c, lanes_of(fluid[t, :, pl.ds(c * L, L)], lane), got)
            for k in range(3):
                f = k * NT + t
                row = f // 6 * 8 + f % 6
                pay[pl.ds(row, 1), span] = jnp.sum(proj[k, :, span] * got, axis=0, keepdims=True)
    pay[pl.ds(27, 1), :] = (node[...] + 1).astype(F32)
    own = owner[...]
    hot = jnp.where(iota((64, 256), 0) == own, 1.0, 0.0)
    before = jnp.where(iota((256, 256), 0) < iota((256, 256), 1), 1.0, 0.0).astype(BF16)
    counts = jnp.dot(hot.astype(BF16), before, preferred_element_type=F32)
    rank = jnp.sum(hot * counts, axis=0, keepdims=True)
    slot = own * CAP + rank.astype(jnp.int32)
    slot_hot = jnp.where(iota((1024, 256), 0) == slot, 1.0, 0.0).astype(BF16)
    slotted = dot_nt(thirds(pay[...]), slot_hot)
    slotted = slotted[0:32] + slotted[32:64] + slotted[64:96]

    part = phase[0] * fluid[0]
    for t in range(1, NT):
        part = part + phase[t] * fluid[t]
    part = jnp.sum(part, axis=0, keepdims=True)
    part = part[:, 0:L] + part[:, L : 2 * L] + part[:, 2 * L : 3 * L] + part[:, 3 * L : 4 * L]
    part = part + pltpu.roll(part, 64, 1)
    part = part + pltpu.roll(part, 32, 1)
    is_phase = iota((8, L), 0) == 4
    place = iota((8, L), 1) >> 5
    for c in range(8):
        groups = [slotted[g * 8 : g * 8 + 8, c * L : c * L + L] for g in range(4)]
        groups[3] = jnp.where(is_phase, part, groups[3])
        turned = []
        for d in range(4):
            mixed = groups[d]
            for j in range(1, 4):
                mixed = jnp.where(place == j, groups[(j + d) % 4], mixed)
            turned.append(pltpu.roll(mixed, 32 * d, 1) if d else mixed)
        for j in range(4):
            packed = turned[(0 - j) % 4]
            for g in range(1, 4):
                packed = jnp.where(place == g, turned[(g - j) % 4], packed)
            base = (c * 4 + j) * ROWS
            for k in range(3):
                out[pl.ds(base + k * NT, NT), :] = struct[k]
            out[pl.ds(base + 21, 6), :] = packed[0:6]


def window_kernel(
    fluid, before, after, jac, nbr, freq, struct, stiff, mass, scal, flux, part, gathered
):
    omega, dfreq = scal[0], scal[1]
    for i in range(4):
        span = pl.ds(i * L, L)
        for f in range(NF):
            off = jnp.broadcast_to(nbr[pl.ds(f, 1), span], (8, L))
            place = iota((8, L), 1) + L + off
            lane = place & (L - 1)
            which = jnp.where(off == 0, 3, place >> 7)
            for t in range(NT):
                got = jnp.zeros((8, L), F32)
                for q in range(3):
                    j = i + q
                    if j == 0:
                        src = before[t]
                    elif j == 5:
                        src = after[t]
                    else:
                        src = fluid[t, :, pl.ds((j - 1) * L, L)]
                    got = jnp.where(which == q, lanes_of(src, lane), got)
                gathered[f, t] = got
        low_half = [(iota((8, L), 0) & s) == 0 for s in (4, 2, 1)]
        for t in range(NT):
            here = fluid[t, :, span]
            sums = [None] * 8
            for f in range(NF + 1):
                val = here if f == 0 else gathered[f - 1, t]
                for vv in range(4):
                    pair = jac[f, pl.ds(vv * 16, 16), span].astype(F32)
                    for u in range(2):
                        term = pair[u * 8 : u * 8 + 8] * val
                        v = vv * 2 + u
                        sums[v] = term if sums[v] is None else sums[v] + term
            level = sums
            for s, low in zip((4, 2, 1), low_half):
                half = len(level) // 2
                level = [
                    jnp.where(
                        low,
                        level[v] + pltpu.roll(level[v], 8 - s, 0),
                        level[v + half] + pltpu.roll(level[v + half], s, 0),
                    )
                    for v in range(half)
                ]
            total = level[0]
            turn = None
            for s in range(NT):
                if s != t:
                    term = float(SPECTRAL[t, s]) * fluid[s, :, span]
                    turn = term if turn is None else turn + term
            flux[t, :, span] = total + omega * turn + dfreq * freq[t, :, span]
    for k in range(3):
        acc = None
        for q in range(3):
            term = dot_nt(struct[q], stiff[k, q], lax.Precision.HIGHEST)
            acc = term if acc is None else acc + term
        for t in range(NT):
            turn = None
            for s in range(NT):
                term = float(SECOND[t, s]) * struct[k, pl.ds(s, 1), :]
                turn = term if turn is None else turn + term
            part[k, pl.ds(t, 1), :] = acc[t : t + 1] + omega * omega * mass[pl.ds(k, 1), :] * turn


def lookup_kernel(mine, other, owner, node, xyz, core, out):
    q = core[0]
    for h in range(2):
        span = pl.ds(h * L, L)
        own = jnp.broadcast_to(owner[:, span], (8, L))
        lane = jnp.broadcast_to(node[:, span], (8, L))
        chip = own >> 1
        same = (own & 1) == q
        found = [jnp.zeros((8, L), F32) for _ in range(3)]
        for table, key in (
            (mine, jnp.where(same, chip, -1)),
            (other, jnp.where(same, -1, chip)),
        ):
            for p in range(CHIPS):
                hit = key == p
                for k in range(3):
                    values = table[pl.ds(p * ROWS + k * NT, 8), :]
                    found[k] = jnp.where(hit, lanes_of(values, lane), found[k])
        last = iota((8, L), 0) == 7
        for k in range(3):
            centre = jnp.broadcast_to(xyz[pl.ds(k, 1), span], (8, L))
            out[pl.ds(k * 8, 8), span] = jnp.where(last, centre, found[k])
    sums = []
    for table in (mine, other):
        acc = table[pl.ds(25, 1), :]
        for p in range(1, CHIPS):
            acc = acc + table[pl.ds(p * ROWS + 25, 1), :]
        sums.append(acc)
    total = jnp.broadcast_to(sums[0] + sums[1], (8, L))
    out[pl.ds(24, 8), pl.ds(0, L)] = total
    out[pl.ds(24, 8), pl.ds(L, L)] = total


def loads_kernel(mine, other, part, core, out, dense):
    q = core[0]
    block = iota((8, L), 1) >> 4
    for a, table in enumerate((mine, other)):
        for c in range(4):
            shifted = []
            for i in range(8):
                values = table[pl.ds((c * 8 + i) * ROWS + 19, 8), :]
                shifted.append(jnp.where(q == 1, pltpu.roll(values, L - 16, 1), values))
            for g in range(4):
                packed = None
                for i in range(8):
                    turn = (16 * i - 32 * g) % L
                    moved = pltpu.roll(shifted[i], turn, 1) if turn else shifted[i]
                    packed = moved if packed is None else jnp.where(block == i, moved, packed)
                dense[pl.ds(g * 8, 8), pl.ds((a * 4 + c) * L, L)] = packed
    tags = dense[pl.ds(29, 1), :].astype(jnp.int32)
    node_hot = jnp.where(iota((L, 1024), 0) + 1 == tags, 1.0, 0.0).astype(BF16)
    loads = dot_nt(thirds(dense[...]), node_hot)
    loads = loads[0:32] + loads[32:64] + loads[64:96]
    for k in range(3):
        for t in range(NT):
            f = k * NT + t
            row = f // 6 * 8 + f % 6 + 2
            out[k, pl.ds(t, 1), :] = part[k, pl.ds(t, 1), :] - loads[row : row + 1]


def parts_of(values):
    high = values.astype(BF16).astype(F32)
    rest = values - high
    middle = rest.astype(BF16).astype(F32)
    return high, middle, rest - middle


def features(xyz, scale, ones_first, out):
    at = 0
    square = None
    for point in xyz:
        square = point * point if square is None else square + point * point
        p = [scale * part for part in parts_of(point)]
        order = (0, 0, 1, 1, 0, 2) if ones_first else (0, 1, 0, 1, 2, 0)
        for i in order:
            out[pl.ds(at, 1), :] = p[i]
            at += 1
    one = jnp.ones_like(square)
    squares = list(parts_of(square))
    for row in [one] * 3 + squares if ones_first else squares + [one] * 3:
        out[pl.ds(at, 1), :] = row
        at += 1
    out[pl.ds(24, 8), :] = jnp.zeros((8, square.shape[1]), F32)


def move_by(ref, cols, rows, squared, basis):
    features([ref[pl.ds(k * 8 + 7, 1), :] for k in range(3)], -2.0, True, rows)
    squared[...] = jnp.dot(cols, rows[...].astype(BF16), preferred_element_type=F32)
    for c in range(8):
        span = pl.ds(c * 64, 64)
        gap = jnp.maximum(squared[span, :], 1e-30)
        dist = gap * lax.rsqrt(gap)
        fall = jnp.maximum(1.0 - dist, 0.0)
        fall = fall * fall
        value = fall * fall * (4.0 * dist + 1.0)
        high = value.astype(BF16)
        basis[span, pl.ds(0, 256)] = high
        basis[span, pl.ds(256, 256)] = (value - high.astype(F32)).astype(BF16)
    shift = ref[pl.ds(0, 24), :]
    high = shift.astype(BF16).astype(F32)
    both = jnp.concatenate([high, shift - high], axis=0).astype(BF16)
    low = jnp.concatenate([high, jnp.zeros_like(high)], axis=0).astype(BF16)
    return dot_nt(basis[...], jnp.concatenate([both, low], axis=1))


def own_kernel(d0, cells, cols, moved, feats, rows, squared, basis):
    features([cells[pl.ds(k, 1), :] for k in range(3)], 1.0, False, feats)
    turned = feats[...].T
    cols[...] = turned
    moved[...] = move_by(d0, turned.astype(BF16), rows, squared, basis)


def final_kernel(d0, d1, d2, d3, cols, moved, sens, flux, out, phase_out, *scratch):
    near = cols[...].astype(BF16)
    total = moved[...]
    for i, ref in enumerate((d1, d3, d2)):
        total = total + move_by(ref, near, *scratch[3 * i : 3 * i + 3])
    turned = total.T
    motion = turned[0:24] + turned[24:48]
    for t in range(NT):
        total = flux[t]
        for k in range(3):
            total = total + sens[k] * motion[k * 8 + t : k * 8 + t + 1]
        out[t] = total
    row = pl.ds(24, 1), pl.ds(0, L)
    total = (d0[row] + d2[row]) + (d1[row] + d3[row])
    total = jnp.where(iota((1, L), 1) >= 96, total, 0.0)
    phase_out[0, 0] = jnp.sum(total)


VM = pl.BlockSpec(memory_space=pltpu.VMEM)
HBM = pl.BlockSpec(memory_space=pltpu.HBM)
SM = pl.BlockSpec(memory_space=pltpu.SMEM)


def kernel(body, name, ins, shapes, outs=None, scratch=(), size=100000, vmem=32):
    return pl.pallas_call(
        body,
        out_shape=[jax.ShapeDtypeStruct(s, F32) for s in shapes],
        in_specs=ins,
        out_specs=outs or [VM] * len(shapes),
        scratch_shapes=list(scratch),
        name=name,
        compiler_params=pltpu.CompilerParams(vmem_limit_bytes=vmem * 1024 * 1024),
        cost_estimate=pl.CostEstimate(flops=1000, bytes_accessed=size, transcendentals=0),
    )


def on_device(
    fluid_delta,
    jacobian,
    face_nbr,
    freq_col,
    grid_sens,
    cell_xyz,
    surf_cell,
    surf_owner,
    surf_node,
    load_proj,
    surf_xyz,
    struct_delta,
    stiffness,
    mass,
    omega,
    freq_delta,
    phase_row,
):
    sections = lax.axis_size("sec")
    columns = lax.axis_size("cell")
    both = sections * columns
    struct = jnp.transpose(struct_delta, (1, 0, 2))
    stiff = jnp.transpose(stiffness, (0, 2, 1, 3))
    sens = jnp.transpose(grid_sens, (1, 0, 2))
    owner = surf_owner.reshape(1, 256)
    node = surf_node.reshape(1, 256)
    cell = surf_cell.reshape(1, 256)
    core = (lax.axis_index("sec") % 2).astype(jnp.int32).reshape(1)
    scal = jnp.concatenate([omega, freq_delta])

    (message,) = kernel(
        prep_kernel,
        "prep",
        [HBM] * 7,
        [(CHIPS * ROWS, L)],
        scratch=[
            pltpu.VMEM((32, 256), F32),
            pltpu.VMEM((NT, NV, 512), F32),
            pltpu.VMEM((NT, NV, 512), F32),
            pltpu.VMEM((1, 256), jnp.int32),
            pltpu.VMEM((1, 256), jnp.int32),
            pltpu.VMEM((1, 256), jnp.int32),
            pltpu.VMEM((3, NV, 256), F32),
            pltpu.VMEM((3, NT, L), F32),
            pltpu.SemaphoreType.DMA((7,)),
        ],
        vmem=60,
    )(fluid_delta, phase_row, cell, owner, node, load_proj, struct)
    groups = [[2 * i + c for i in range(sections // 2)] for c in range(2)]
    mine = lax.all_to_all(
        message.reshape(CHIPS, 1, ROWS * L), "sec", 0, 0, axis_index_groups=groups, tiled=True
    ).reshape(CHIPS * ROWS, L)
    up = [(i, i + 1) for i in range(both - 1)]
    down = [(i + 1, i) for i in range(both - 1)]
    before = lax.ppermute(fluid_delta[:, :, 3 * L :], ("sec", "cell"), up)
    after = lax.ppermute(fluid_delta[:, :, :L], ("sec", "cell"), down)
    flux, part = kernel(
        window_kernel,
        "window",
        [VM] * 9 + [SM],
        [(NT, NV, 512), (3, NT, L)],
        scratch=[pltpu.VMEM((NF, NT, 8, L), F32)],
        size=4 * 10**6,
    )(
        fluid_delta,
        before,
        after,
        jacobian.reshape(NF + 1, 64, 512),
        face_nbr,
        freq_col,
        struct,
        stiff,
        mass,
        scal,
    )
    mine, flux, part = lax.optimization_barrier((mine, flux, part))
    other = lax.ppermute(mine, "sec", [(i, i ^ 1) for i in range(sections)])
    (disp,) = kernel(lookup_kernel, "lookup", [VM] * 5 + [SM], [(32, 256)])(
        mine, other, owner, node, surf_xyz, core
    )
    d1, d3, d2 = (
        lax.ppermute(disp, "cell", [(i, (i + k) % columns) for i in range(columns)])
        for k in (1, 3, 2)
    )
    (struct_out,) = kernel(
        loads_kernel,
        "loads",
        [VM] * 3 + [SM],
        [(3, NT, L)],
        scratch=[pltpu.VMEM((32, 1024), F32)],
        size=2 * 10**6,
    )(mine, other, part, core)
    move = [
        pltpu.VMEM((32, 256), F32),
        pltpu.VMEM((512, 256), F32),
        pltpu.VMEM((512, 512), BF16),
    ]
    cols, moved = kernel(
        own_kernel,
        "own",
        [VM] * 2,
        [(512, 32), (512, 48)],
        scratch=[pltpu.VMEM((32, 512), F32)] + move,
        size=2 * 10**6,
    )(disp, cell_xyz)
    fluid_out, phase_out = kernel(
        final_kernel,
        "final",
        [VM] * 8,
        [(NT, NV, 512), (1, 1)],
        outs=[VM, SM],
        scratch=move * 3,
    )(disp, d1, d2, d3, cols, moved, sens, flux)
    return fluid_out, jnp.transpose(struct_out, (1, 0, 2)), phase_out.reshape(1)


def solution(mesh):
    split = ("sec", "cell")
    return jax.shard_map(
        on_device,
        mesh=mesh,
        in_specs=(
            P(None, None, split),
            P(None, None, None, split),
            P(None, split),
            P(None, None, split),
            P(None, None, split),
            P(None, split),
            P(split),
            P(split, None),
            P(split),
            P(None, None, split),
            P(None, split),
            P(None, None, split),
            P(None, None, None, split),
            P(None, split),
            P(),
            P(),
            P(None, None, split),
        ),
        out_specs=(P(None, None, split), P(None, None, split), P()),
        check_vma=False,
    )
```

```python
import functools

import jax
import jax.numpy as jnp
import numpy as np
from jax import lax
from jax.experimental import pallas as pl
from jax.experimental.pallas import tpu as pltpu
from jax.sharding import PartitionSpec as P

NT = 7
NV = 8
NF = 6
L = 128
CHIPS = 32
CAP = 16
ROWS = 27
F32 = jnp.float32
BF16 = jnp.bfloat16


def spectral_table(instances):
    positions = np.arange(instances)
    offset = positions[:, None] - positions[None, :]
    clipped = np.where(offset == 0, 1, offset)
    return np.where(
        offset == 0, 0.0, 0.5 * (-1.0) ** offset / np.sin(np.pi * clipped / instances)
    )


SPECTRAL = np.asarray(spectral_table(NT), np.float32)
SECOND = np.asarray(spectral_table(NT) @ spectral_table(NT), np.float32)


def iota(shape, axis):
    return lax.broadcasted_iota(jnp.int32, shape, axis)


def lanes_of(values, index):
    return jnp.take_along_axis(values, index, axis=1, mode="promise_in_bounds")


def thirds(values):
    high = values.astype(BF16)
    rest = values - high.astype(F32)
    middle = rest.astype(BF16)
    low = (rest - middle.astype(F32)).astype(BF16)
    return jnp.concatenate([high, middle, low], axis=0)


def dot_nt(a, b, precision=None):
    return lax.dot_general(
        a, b, (((1,), (1,)), ((), ())), precision=precision, preferred_element_type=F32
    )


def prep_kernel(*refs):
    far, out, tags, near = refs[:11], refs[11], refs[12], refs[13:24]
    pay, message, tag_rows, sems, out_sems = refs[24:]
    fluid, phase, cell, owner, node, proj, struct, xyz, nbr, mass, cells = near
    copies = [pltpu.make_async_copy(a, b, sems.at[i]) for i, (a, b) in enumerate(zip(far, near))]
    for i in (3, 4, 2, 0, 5, 6, 7, 8, 9, 10, 1):
        copies[i].start()
    pay[...] = jnp.zeros_like(pay)
    copies[3].wait()
    own = owner[...]
    hot = jnp.where(iota((64, 256), 0) == own, 1.0, 0.0)
    before = jnp.where(iota((256, 256), 0) < iota((256, 256), 1), 1.0, 0.0).astype(BF16)
    counts = jnp.dot(hot.astype(BF16), before, preferred_element_type=F32)
    rank = jnp.sum(hot * counts, axis=0, keepdims=True)
    slot = own * CAP + rank.astype(jnp.int32)
    slot_hot = jnp.where(iota((1024, 256), 0) == slot, 1.0, 0.0).astype(BF16)
    copies[4].wait()
    pay[pl.ds(27, 1), :] = (node[...] + 1).astype(F32)
    copies[2].wait()
    copies[6].wait()
    for p in range(CHIPS):
        for k in range(3):
            message[pl.ds(p * ROWS + k * NT, NT), :] = struct[k]
    copies[0].wait()
    copies[5].wait()
    for i in range(7, 11):
        copies[i].wait()
    tag_rows[...] = jnp.zeros_like(tag_rows)
    tag_rows[pl.ds(0, 1), :] = own.astype(F32)
    tag_rows[pl.ds(1, 1), :] = node[...].astype(F32)
    tag_rows[pl.ds(2, 3), :] = xyz[...]
    for k in range(3):
        tag_rows[pl.ds(32 + k * 8, NT), pl.ds(0, L)] = struct[k]
    tag_rows[pl.ds(8, 3), pl.ds(0, L)] = mass[...]
    for h in range(2):
        half = pl.ds(h * 256, 256)
        tag_rows[pl.ds(11 + 6 * h, 6), :] = nbr[:, half].astype(F32)
        tag_rows[pl.ds(23 + 3 * h, 3), :] = cells[:, half]
    sent = [pltpu.make_async_copy(tag_rows, tags, out_sems.at[4])]
    sent[0].start()
    for h in range(2):
        span = pl.ds(h * L, L)
        index = jnp.broadcast_to(cell[:, span], (8, L))
        lane, chunk = index & (L - 1), index >> 7
        for t in range(NT):
            got = lanes_of(fluid[t, :, pl.ds(0, L)], lane)
            for c in range(1, 4):
                got = jnp.where(chunk == c, lanes_of(fluid[t, :, pl.ds(c * L, L)], lane), got)
            for k in range(3):
                f = k * NT + t
                row = f // 6 * 8 + f % 6
                pay[pl.ds(row, 1), span] = jnp.sum(proj[k, :, span] * got, axis=0, keepdims=True)
    slotted = dot_nt(thirds(pay[...]), slot_hot)
    slotted = slotted[0:32] + slotted[32:64] + slotted[64:96]

    copies[1].wait()
    part = phase[0] * fluid[0]
    for t in range(1, NT):
        part = part + phase[t] * fluid[t]
    part = jnp.sum(part, axis=0, keepdims=True)
    part = part[:, 0:L] + part[:, L : 2 * L] + part[:, 2 * L : 3 * L] + part[:, 3 * L : 4 * L]
    part = part + pltpu.roll(part, 64, 1)
    part = part + pltpu.roll(part, 32, 1)
    is_phase = iota((8, L), 0) == 4
    place = iota((8, L), 1) >> 5
    for c in range(8):
        groups = [slotted[g * 8 : g * 8 + 8, c * L : c * L + L] for g in range(4)]
        groups[3] = jnp.where(is_phase, part, groups[3])
        turned = []
        for d in range(4):
            mixed = groups[d]
            for j in range(1, 4):
                mixed = jnp.where(place == j, groups[(j + d) % 4], mixed)
            turned.append(pltpu.roll(mixed, 32 * d, 1) if d else mixed)
        for j in range(4):
            packed = turned[(0 - j) % 4]
            for g in range(1, 4):
                packed = jnp.where(place == g, turned[(g - j) % 4], packed)
            message[pl.ds((c * 4 + j) * ROWS + 21, 6), :] = packed[0:6]
        if c % 2:
            span = pl.ds((c - 1) * 4 * ROWS, 8 * ROWS)
            copy = pltpu.make_async_copy(message.at[span], out.at[span], out_sems.at[c // 2])
            copy.start()
            sent.append(copy)
    for copy in sent:
        copy.wait()


def sides_kernel(fluid, tags, near, far):
    even = (lax.axis_index("cell") & 1) == 0
    for t in range(NT):
        first, last = fluid[t, :, pl.ds(0, L)], fluid[t, :, pl.ds(3 * L, L)]
        near[pl.ds(t * 8, 8), :] = jnp.where(even, last, first)
        far[t] = jnp.where(even, first, last)
    near[pl.ds(56, 8), :] = tags[pl.ds(0, 8), pl.ds(0, L)]
    near[pl.ds(64, 8), :] = tags[pl.ds(0, 8), pl.ds(L, L)]


def fold(level):
    for s in (4, 2, 1):
        half = len(level) // 2
        low = (iota((8, L), 0) & s) == 0
        level = [
            jnp.where(
                low,
                level[v] + pltpu.roll(level[v], 8 - s, 0),
                level[v + half] + pltpu.roll(level[v + half], s, 0),
            )
            for v in range(half)
        ]
    return level[0]


def gain(sums, jac, f, span, val):
    for vv in range(4):
        pair = jac[f, pl.ds(vv * 16, 16), span].astype(F32)
        for u in range(2):
            term = pair[u * 8 : u * 8 + 8] * val
            v = vv * 2 + u
            sums[v] = term if sums[v] is None else sums[v] + term


def window_kernel(
    fluid,
    near,
    jac,
    stiff,
    tags,
    omega_ref,
    dfreq_ref,
    flux,
    part,
    rate,
    cols,
    basis,
    near_basis,
    gathered,
    feats,
    rows,
    squared,
    rows2,
    squared2,
):
    even = (lax.axis_index("cell") & 1) == 0
    omega = omega_ref[...].reshape(1, 1)
    rate[...] = jnp.broadcast_to(dfreq_ref[...].reshape(1, 1), (8, L))
    for i in range(4):
        span = pl.ds(i * L, L)
        for f in range(NF):
            row = tags[pl.ds(11 + 6 * (i // 2) + f, 1), pl.ds(i % 2 * L, L)]
            off = jnp.broadcast_to(row, (8, L)).astype(jnp.int32)
            place = iota((8, L), 1) + L + off
            lane = place & (L - 1)
            which = jnp.where(off == 0, 3, place >> 7)
            for t in range(NT):
                got = jnp.zeros((8, L), F32)
                for q in range(3):
                    j = i + q
                    if j in (0, 5):
                        src = jnp.where(even == (j == 5), near[pl.ds(t * 8, 8), :], 0.0)
                    else:
                        src = fluid[t, :, pl.ds((j - 1) * L, L)]
                    got = jnp.where(which == q, lanes_of(src, lane), got)
                gathered[f, t] = got
        for t in range(NT):
            here = fluid[t, :, span]
            sums = [None] * 8
            for f in range(NF + 1):
                val = here if f == 0 else gathered[f - 1, t]
                gain(sums, jac, f, span, val)
            total = fold(sums)
            turn = None
            for s in range(NT):
                if s != t:
                    term = float(SPECTRAL[t, s]) * fluid[s, :, span]
                    turn = term if turn is None else turn + term
            flux[t, :, span] = total + omega * turn
    for k in range(3):
        acc = None
        for q in range(3):
            term = dot_nt(tags[pl.ds(32 + q * 8, NT), pl.ds(0, L)], stiff[k, q], lax.Precision.HIGHEST)
            acc = term if acc is None else acc + term
        for t in range(NT):
            turn = None
            for s in range(NT):
                term = float(SECOND[t, s]) * tags[pl.ds(32 + k * 8 + s, 1), pl.ds(0, L)]
                turn = term if turn is None else turn + term
            part[k, pl.ds(t, 1), :] = acc[t : t + 1] + omega * omega * tags[pl.ds(8 + k, 1), pl.ds(0, L)] * turn

    points = [
        jnp.concatenate([tags[pl.ds(23 + k, 1), :], tags[pl.ds(26 + k, 1), :]], axis=1)
        for k in range(3)
    ]
    features(points, 1.0, False, feats)
    turned = feats[...].T
    cols[...] = turned
    centres = [tags[pl.ds(2 + k, 1), :] for k in range(3)]
    basis_of(centres, turned.astype(BF16), rows, squared, basis)
    centres = [
        jnp.concatenate([near[pl.ds(58 + k, 1), :], near[pl.ds(66 + k, 1), :]], axis=1)
        for k in range(3)
    ]
    basis_of(centres, turned.astype(BF16), rows2, squared2, near_basis)


def edge_kernel(far, jac, tags, out):
    even = (lax.axis_index("cell") & 1) == 0
    at = pl.multiple_of(jnp.where(even, 0, 3 * L), L)
    want = jnp.where(even, 0, 2)
    places = []
    for f in range(NF):
        first, last = tags[pl.ds(11 + f, 1), pl.ds(0, L)], tags[pl.ds(17 + f, 1), pl.ds(L, L)]
        off = jnp.broadcast_to(jnp.where(even, first, last), (8, L)).astype(jnp.int32)
        places.append(iota((8, L), 1) + L + off)
    for t in range(NT):
        sums = [None] * 8
        for f in range(NF):
            got = lanes_of(far[t], places[f] & (L - 1))
            val = jnp.where((places[f] >> 7) == want, got, 0.0)
            gain(sums, jac, f + 1, pl.ds(at, L), val)
        out[t] = fold(sums)


def lookup_kernel(table, tags, other_tags, out, far):
    q = lax.axis_index("sec") & 1
    last = iota((8, L), 0) == 7
    total = table[pl.ds(25, 1), :]
    for p in range(1, CHIPS):
        total = total + table[pl.ds(p * ROWS + 25, 1), :]
    total = jnp.broadcast_to(total, (8, L))
    for other, (tag, to) in enumerate(((tags, out), (other_tags, far))):
        for h in range(2):
            span = pl.ds(h * L, L)
            own = jnp.broadcast_to(tag[pl.ds(0, 1), span], (8, L)).astype(jnp.int32)
            lane = jnp.broadcast_to(tag[pl.ds(1, 1), span], (8, L)).astype(jnp.int32)
            key = jnp.where((own & 1) == q, own >> 1, -1)
            found = [jnp.zeros((8, L), F32) for _ in range(3)]
            for p in range(CHIPS):
                hit = key == p
                for k in range(3):
                    values = table[pl.ds(p * ROWS + k * NT, 8), :]
                    found[k] = jnp.where(hit, lanes_of(values, lane), found[k])
            for k in range(3):
                extra = 0.0 if other else jnp.broadcast_to(tag[pl.ds(2 + k, 1), span], (8, L))
                to[pl.ds(h * 32 + k * 8, 8), :] = jnp.where(last, extra, found[k])
            to[pl.ds(h * 32 + 24, 8), :] = total
    for p in range(CHIPS):
        far[pl.ds(64 + p * 8, 8), :] = table[pl.ds(p * ROWS + 19, 8), :]


def node_sums(table, stride, base, dense):
    q = lax.axis_index("sec") & 1
    block = iota((8, L), 1) >> 4
    for c in range(4):
        shifted = []
        for i in range(8):
            values = table[pl.ds((c * 8 + i) * stride + base, 8), :]
            shifted.append(jnp.where(q == 1, pltpu.roll(values, L - 16, 1), values))
        for g in range(4):
            packed = None
            for i in range(8):
                turn = (16 * i - 32 * g) % L
                moved = pltpu.roll(shifted[i], turn, 1) if turn else shifted[i]
                packed = moved if packed is None else jnp.where(block == i, moved, packed)
            dense[pl.ds(g * 8, 8), pl.ds(c * L, L)] = packed
    tags = dense[pl.ds(29, 1), :].astype(jnp.int32)
    node_hot = jnp.where(iota((L, 512), 0) + 1 == tags, 1.0, 0.0).astype(BF16)
    loads = dot_nt(thirds(dense[...]), node_hot)
    return loads[0:32] + loads[32:64] + loads[64:96]


def own_loads_kernel(table, out, dense):
    out[...] = node_sums(table, ROWS, 19, dense)


def loads_kernel(other, sums, part, out, dense):
    loads = node_sums(other, 8, 64, dense) + sums[...]
    for k in range(3):
        for t in range(NT):
            f = k * NT + t
            row = f // 6 * 8 + f % 6 + 2
            out[k, pl.ds(t, 1), :] = part[k, pl.ds(t, 1), :] - loads[row : row + 1]


def parts_of(values):
    high = values.astype(BF16).astype(F32)
    rest = values - high
    middle = rest.astype(BF16).astype(F32)
    return high, middle, rest - middle


def features(xyz, scale, ones_first, out):
    at = 0
    square = None
    for point in xyz:
        square = point * point if square is None else square + point * point
        p = [scale * part for part in parts_of(point)]
        order = (0, 0, 1, 1, 0, 2) if ones_first else (0, 1, 0, 1, 2, 0)
        for i in order:
            out[pl.ds(at, 1), :] = p[i]
            at += 1
    one = jnp.ones_like(square)
    squares = list(parts_of(square))
    for row in [one] * 3 + squares if ones_first else squares + [one] * 3:
        out[pl.ds(at, 1), :] = row
        at += 1
    out[pl.ds(24, 8), :] = jnp.zeros((8, square.shape[1]), F32)


def basis_of(centres, cols, rows, squared, basis):
    features(centres, -2.0, True, rows)
    squared[...] = jnp.dot(cols, rows[...].astype(BF16), preferred_element_type=F32)
    for c in range(8):
        span = pl.ds(c * 64, 64)
        gap = jnp.maximum(squared[span, :], 1e-30)
        dist = gap * lax.rsqrt(gap)
        fall = jnp.maximum(1.0 - dist, 0.0)
        fall = fall * fall
        value = fall * fall * (4.0 * dist + 1.0)
        high = value.astype(BF16)
        basis[span, pl.ds(0, 256)] = high
        basis[span, pl.ds(256, 256)] = (value - high.astype(F32)).astype(BF16)


def halves(ref):
    return jnp.concatenate([ref[pl.ds(0, 24), :], ref[pl.ds(32, 24), :]], axis=1)


def moved_by(both, basis):
    high = both.astype(BF16).astype(F32)
    upper = jnp.concatenate([high, both - high], axis=0).astype(BF16)
    lower = jnp.concatenate([high, jnp.zeros_like(high)], axis=0).astype(BF16)
    return dot_nt(basis[...], jnp.concatenate([upper, lower], axis=1))


def block_of(ref, cols, rows, squared, basis):
    both = halves(ref)
    centres = [both[k * 8 + 7 : k * 8 + 8] for k in range(3)]
    basis_of(centres, cols[...].astype(BF16), rows, squared, basis)
    return moved_by(both, basis)


def first_kernel(d0, d2, cols, own_basis, out, rows, squared, basis):
    out[...] = moved_by(halves(d0), own_basis) + block_of(d2, cols, rows, squared, basis)


def block_kernel(ref, cols, moved, out, rows, squared, basis):
    out[...] = moved[...] + block_of(ref, cols, rows, squared, basis)


def final_kernel(
    d0, d1, d2, d3, near_basis, moved, sens, flux, freq, rate, edge, out, phase_out
):
    total = moved[...] + moved_by(halves(d1), near_basis)
    turned = total.T
    motion = turned[0:24] + turned[24:48]
    for t in range(NT):
        total = flux[t] + rate[pl.ds(0, 1), pl.ds(0, 1)] * freq[t]
        for k in range(3):
            total = total + sens[k] * motion[k * 8 + t : k * 8 + t + 1]
        out[t] = total
    even = (lax.axis_index("cell") & 1) == 0
    span = pl.ds(pl.multiple_of(jnp.where(even, 0, 3 * L), L), L)
    for t in range(NT):
        out[t, :, span] = out[t, :, span] + edge[t]
    row = pl.ds(24, 1), pl.ds(0, L)
    total = (d0[row] + d1[row]) + (d2[row] + d3[row])
    total = jnp.where(iota((1, L), 1) >= 96, total, 0.0)
    phase_out[0, 0] = jnp.sum(total)


VM = pl.BlockSpec(memory_space=pltpu.VMEM)
HBM = pl.BlockSpec(memory_space=pltpu.HBM)
SM = pl.BlockSpec(memory_space=pltpu.SMEM)


def kernel(body, name, ins, shapes, outs=None, types=None, scratch=(), size=100000, vmem=32):
    return pl.pallas_call(
        body,
        out_shape=[
            jax.ShapeDtypeStruct(s, t) for s, t in zip(shapes, types or [F32] * len(shapes))
        ],
        in_specs=ins,
        out_specs=outs or [VM] * len(shapes),
        scratch_shapes=list(scratch),
        name=name,
        compiler_params=pltpu.CompilerParams(vmem_limit_bytes=vmem * 1024 * 1024),
        cost_estimate=pl.CostEstimate(flops=1000, bytes_accessed=size, transcendentals=0),
    )


def on_device(
    fluid_delta,
    jacobian,
    face_nbr,
    freq_col,
    grid_sens,
    cell_xyz,
    surf_cell,
    surf_owner,
    surf_node,
    load_proj,
    surf_xyz,
    struct_delta,
    stiffness,
    mass,
    omega,
    freq_delta,
    phase_row,
):
    sections = lax.axis_size("sec")
    columns = lax.axis_size("cell")
    both = sections * columns
    struct = jnp.transpose(struct_delta, (1, 0, 2))
    stiff = jnp.transpose(stiffness, (0, 2, 1, 3))
    jac = jacobian.reshape(NF + 1, 64, 512)
    sens = jnp.transpose(grid_sens, (1, 0, 2))
    owner = surf_owner.reshape(1, 256)
    node = surf_node.reshape(1, 256)
    cell = surf_cell.reshape(1, 256)

    message, tags = kernel(
        prep_kernel,
        "prep",
        [HBM] * 11,
        [(CHIPS * ROWS, L), (56, 256)],
        outs=[HBM] * 2,
        scratch=[
            pltpu.VMEM((NT, NV, 512), F32),
            pltpu.VMEM((NT, NV, 512), F32),
            pltpu.VMEM((1, 256), jnp.int32),
            pltpu.VMEM((1, 256), jnp.int32),
            pltpu.VMEM((1, 256), jnp.int32),
            pltpu.VMEM((3, NV, 256), F32),
            pltpu.VMEM((3, NT, L), F32),
            pltpu.VMEM((3, 256), F32),
            pltpu.VMEM((NF, 512), jnp.int32),
            pltpu.VMEM((3, L), F32),
            pltpu.VMEM((3, 512), F32),
            pltpu.VMEM((32, 256), F32),
            pltpu.VMEM((CHIPS * ROWS, L), F32),
            pltpu.VMEM((56, 256), F32),
            pltpu.SemaphoreType.DMA((11,)),
            pltpu.SemaphoreType.DMA((5,)),
        ],
        vmem=60,
    )(
        fluid_delta,
        phase_row,
        cell,
        owner,
        node,
        load_proj,
        struct,
        surf_xyz,
        face_nbr,
        mass,
        cell_xyz,
    )
    groups = [[2 * i + c for i in range(sections // 2)] for c in range(2)]
    mine = lax.all_to_all(
        message.reshape(CHIPS, 1, ROWS * L), "sec", 0, 0, axis_index_groups=groups, tiled=True
    ).reshape(CHIPS * ROWS, L)
    swap = [(i, i ^ 1) for i in range(sections)]
    other_tags = lax.ppermute(tags, "sec", swap)
    pairs = [[(i, i ^ 1) for i in range(both)], [(i, ((i + 1) ^ 1) - 1) for i in range(1, both - 1)]]
    near_side, far_side = kernel(sides_kernel, "sides", [VM] * 2, [(72, L), (NT, NV, L)])(
        fluid_delta, tags
    )
    near_edge = lax.ppermute(near_side, ("sec", "cell"), pairs[0])
    far_edge = lax.ppermute(far_side, ("sec", "cell"), pairs[1])
    move = [
        pltpu.VMEM((32, 256), F32),
        pltpu.VMEM((512, 256), F32),
    ]
    flux, part, rate, cols, own_basis, near_basis = kernel(
        window_kernel,
        "window",
        [VM] * 7,
        [(NT, NV, 512), (3, NT, L), (8, L), (512, 32), (512, 512), (512, 512)],
        types=[F32] * 4 + [BF16] * 2,
        scratch=[pltpu.VMEM((NF, NT, 8, L), F32), pltpu.VMEM((32, 512), F32)] + move * 2,
        size=4 * 10**6,
    )(
        fluid_delta,
        near_edge,
        jac,
        stiff,
        tags,
        omega,
        freq_delta,
    )
    (edge,) = kernel(edge_kernel, "edge", [VM] * 3, [(NT, NV, L)])(far_edge, jac, tags)
    mine, flux, edge = lax.optimization_barrier((mine, flux, edge))
    near, far = kernel(lookup_kernel, "lookup", [VM] * 3, [(64, L), (320, L)])(
        mine, tags, other_tags
    )
    back = lax.ppermute(far, "sec", swap)
    (sums,) = kernel(
        own_loads_kernel, "own_loads", [VM], [(32, L)], scratch=[pltpu.VMEM((32, 512), F32)]
    )(mine)
    back, sums = lax.optimization_barrier((back, sums))
    disp = near + back[:64]
    d2, d3, d1 = (
        lax.ppermute(disp, "cell", [(i, i ^ k) for i in range(columns)]) for k in (2, 3, 1)
    )
    (struct_out,) = kernel(
        loads_kernel,
        "loads",
        [VM] * 3,
        [(3, NT, L)],
        scratch=[pltpu.VMEM((32, 512), F32)],
        size=2 * 10**6,
    )(back, sums, part)
    move.append(pltpu.VMEM((512, 512), BF16))
    struct_out, d2 = lax.optimization_barrier((struct_out, d2))
    (moved,) = kernel(
        first_kernel, "first", [VM] * 4, [(512, 48)], scratch=move, size=2 * 10**6
    )(disp, d2, cols, own_basis)
    (moved,) = kernel(
        block_kernel, "block", [VM] * 3, [(512, 48)], scratch=move, size=2 * 10**6
    )(d3, cols, moved)
    fluid_out, phase_out = kernel(
        final_kernel,
        "final",
        [VM] * 11,
        [(NT, NV, 512), (1, 1)],
        outs=[VM, SM],
    )(disp, d1, d2, d3, near_basis, moved, sens, flux, freq_col, rate, edge)
    return fluid_out, jnp.transpose(struct_out, (1, 0, 2)), phase_out.reshape(1)


def solution(mesh):
    split = ("sec", "cell")
    return jax.shard_map(
        on_device,
        mesh=mesh,
        in_specs=(
            P(None, None, split),
            P(None, None, None, split),
            P(None, split),
            P(None, None, split),
            P(None, None, split),
            P(None, split),
            P(split),
            P(split, None),
            P(split),
            P(None, None, split),
            P(None, split),
            P(None, None, split),
            P(None, None, None, split),
            P(None, split),
            P(),
            P(),
            P(None, None, split),
        ),
        out_specs=(P(None, None, split), P(None, None, split), P()),
        check_vma=False,
    )
```

```python
import functools

import jax
import jax.numpy as jnp
import numpy as np
from jax import lax
from jax.experimental import pallas as pl
from jax.experimental.pallas import tpu as pltpu
from jax.sharding import PartitionSpec as P

NT = 7
NV = 8
NF = 6
L = 128
CHIPS = 32
CAP = 16
ROWS = 27
RUNS = ((0, 0, 6, 2), (0, 6, 1, 10), (1, 0, 5, 11), (1, 5, 2, 18), (2, 0, 4, 20), (2, 4, 3, 26))
F32 = jnp.float32
BF16 = jnp.bfloat16


def spectral_table(instances):
    positions = np.arange(instances)
    offset = positions[:, None] - positions[None, :]
    clipped = np.where(offset == 0, 1, offset)
    return np.where(
        offset == 0, 0.0, 0.5 * (-1.0) ** offset / np.sin(np.pi * clipped / instances)
    )


SPECTRAL = np.asarray(spectral_table(NT), np.float32)
SECOND = np.asarray(spectral_table(NT) @ spectral_table(NT), np.float32)


def iota(shape, axis):
    return lax.broadcasted_iota(jnp.int32, shape, axis)


def lanes_of(values, index):
    return jnp.take_along_axis(values, index, axis=1, mode="promise_in_bounds")


def thirds(values):
    high = values.astype(BF16)
    rest = values - high.astype(F32)
    middle = rest.astype(BF16)
    low = (rest - middle.astype(F32)).astype(BF16)
    return jnp.concatenate([high, middle, low], axis=0)


def dot_nt(a, b, precision=None):
    return lax.dot_general(
        a, b, (((1,), (1,)), ((), ())), precision=precision, preferred_element_type=F32
    )


def prep_kernel(*refs):
    far, out, tags, near = refs[:11], refs[11], refs[12], refs[13:24]
    pay, message, sems, out_sems = refs[24:]
    tag_rows, sent = tags, []
    fluid, phase, cell, owner, node, proj, struct, xyz, nbr, mass, cells = near
    copies = [pltpu.make_async_copy(a, b, sems.at[i]) for i, (a, b) in enumerate(zip(far, near))]
    for i in (3, 4, 2, 0, 5, 6, 7, 8, 9, 10, 1):
        copies[i].start()
    pay[...] = jnp.zeros_like(pay)
    copies[3].wait()
    own = owner[...]
    hot = jnp.where(iota((64, 256), 0) == own, 1.0, 0.0)
    before = jnp.where(iota((256, 256), 0) < iota((256, 256), 1), 1.0, 0.0).astype(BF16)
    counts = jnp.dot(hot.astype(BF16), before, preferred_element_type=F32)
    rank = jnp.sum(hot * counts, axis=0, keepdims=True)
    slot = own * CAP + rank.astype(jnp.int32)
    slot_hot = jnp.where(iota((1024, 256), 0) == slot, 1.0, 0.0).astype(BF16)
    copies[4].wait()
    pay[pl.ds(27, 1), :] = (node[...] + 1).astype(F32)
    copies[2].wait()
    copies[6].wait()
    for p in range(CHIPS):
        for k in range(3):
            message[pl.ds(p * ROWS + k * NT, NT), :] = struct[k]
    copies[0].wait()
    copies[5].wait()
    for i in range(7, 11):
        copies[i].wait()
    tag_rows[...] = jnp.zeros_like(tag_rows)
    tag_rows[pl.ds(0, 1), :] = own.astype(F32)
    tag_rows[pl.ds(1, 1), :] = node[...].astype(F32)
    tag_rows[pl.ds(2, 3), :] = xyz[...]
    for k in range(3):
        tag_rows[pl.ds(32 + k * 8, NT), pl.ds(0, L)] = struct[k]
    tag_rows[pl.ds(8, 3), pl.ds(0, L)] = mass[...]
    for h in range(2):
        half = pl.ds(h * 256, 256)
        tag_rows[pl.ds(11 + 6 * h, 6), :] = nbr[:, half].astype(F32)
        tag_rows[pl.ds(23 + 3 * h, 3), :] = cells[:, half]
    for h in range(2):
        span = pl.ds(h * L, L)
        index = jnp.broadcast_to(cell[:, span], (8, L))
        lane, chunk = index & (L - 1), index >> 7
        for t in range(NT):
            got = lanes_of(fluid[t, :, pl.ds(0, L)], lane)
            for c in range(1, 4):
                got = jnp.where(chunk == c, lanes_of(fluid[t, :, pl.ds(c * L, L)], lane), got)
            for k in range(3):
                f = k * NT + t
                row = f // 6 * 8 + f % 6
                pay[pl.ds(row, 1), span] = jnp.sum(proj[k, :, span] * got, axis=0, keepdims=True)
    slotted = dot_nt(thirds(pay[...]), slot_hot)
    slotted = slotted[0:32] + slotted[32:64] + slotted[64:96]

    copies[1].wait()
    part = phase[0] * fluid[0]
    for t in range(1, NT):
        part = part + phase[t] * fluid[t]
    part = jnp.sum(part, axis=0, keepdims=True)
    part = part[:, 0:L] + part[:, L : 2 * L] + part[:, 2 * L : 3 * L] + part[:, 3 * L : 4 * L]
    part = part + pltpu.roll(part, 64, 1)
    part = part + pltpu.roll(part, 32, 1)
    is_phase = iota((8, L), 0) == 4
    place = iota((8, L), 1) >> 5
    for c in range(8):
        groups = [slotted[g * 8 : g * 8 + 8, c * L : c * L + L] for g in range(4)]
        groups[3] = jnp.where(is_phase, part, groups[3])
        turned = []
        for d in range(4):
            mixed = groups[d]
            for j in range(1, 4):
                mixed = jnp.where(place == j, groups[(j + d) % 4], mixed)
            turned.append(pltpu.roll(mixed, 32 * d, 1) if d else mixed)
        for j in range(4):
            packed = turned[(0 - j) % 4]
            for g in range(1, 4):
                packed = jnp.where(place == g, turned[(g - j) % 4], packed)
            message[pl.ds((c * 4 + j) * ROWS + 21, 6), :] = packed[0:6]
        if c % 2:
            span = pl.ds((c - 1) * 4 * ROWS, 8 * ROWS)
            copy = pltpu.make_async_copy(message.at[span], out.at[span], out_sems.at[c // 2])
            copy.start()
            sent.append(copy)
    for copy in sent:
        copy.wait()


def sides_kernel(fluid, tags, near, far, centres):
    even = (lax.axis_index("cell") & 1) == 0
    for t in range(NT):
        first, last = fluid[t, :, pl.ds(0, L)], fluid[t, :, pl.ds(3 * L, L)]
        near[pl.ds(t * 8, 8), :] = jnp.where(even, last, first)
        far[t] = jnp.where(even, first, last)
    for h in range(2):
        near[pl.ds(56 + 8 * h, 8), :] = tags[pl.ds(0, 8), pl.ds(h * L, L)]
        centres[pl.ds(8 * h, 8), :] = tags[pl.ds(0, 8), pl.ds(h * L, L)]


def fold(level):
    for s in (4, 2, 1):
        half = len(level) // 2
        low = (iota((8, L), 0) & s) == 0
        level = [
            jnp.where(
                low,
                level[v] + pltpu.roll(level[v], 8 - s, 0),
                level[v + half] + pltpu.roll(level[v + half], s, 0),
            )
            for v in range(half)
        ]
    return level[0]


def gain(sums, jac, f, span, val):
    for vv in range(4):
        pair = jac[f, pl.ds(vv * 16, 16), span].astype(F32)
        for u in range(2):
            term = pair[u * 8 : u * 8 + 8] * val
            v = vv * 2 + u
            sums[v] = term if sums[v] is None else sums[v] + term


def window_kernel(
    fluid,
    near,
    centres3,
    jac,
    freq,
    stiff,
    tags,
    omega_ref,
    dfreq_ref,
    flux,
    part,
    kept,
    basis0,
    basis1,
    basis3,
    gathered,
    feats,
    rows,
    squared,
):
    even = (lax.axis_index("cell") & 1) == 0
    omega = omega_ref[...].reshape(1, 1)
    dfreq = dfreq_ref[...].reshape(1, 1)
    for i in range(4):
        span = pl.ds(i * L, L)
        for f in range(NF):
            row = tags[pl.ds(11 + 6 * (i // 2) + f, 1), pl.ds(i % 2 * L, L)]
            off = jnp.broadcast_to(row, (8, L)).astype(jnp.int32)
            place = iota((8, L), 1) + L + off
            lane = place & (L - 1)
            which = jnp.where(off == 0, 3, place >> 7)
            for t in range(NT):
                got = jnp.zeros((8, L), F32)
                for q in range(3):
                    j = i + q
                    if j in (0, 5):
                        src = jnp.where(even == (j == 5), near[pl.ds(t * 8, 8), :], 0.0)
                    else:
                        src = fluid[t, :, pl.ds((j - 1) * L, L)]
                    got = jnp.where(which == q, lanes_of(src, lane), got)
                gathered[f, t] = got
        for t in range(NT):
            here = fluid[t, :, span]
            sums = [None] * 8
            for f in range(NF + 1):
                val = here if f == 0 else gathered[f - 1, t]
                gain(sums, jac, f, span, val)
            total = fold(sums)
            turn = None
            for s in range(NT):
                if s != t:
                    term = float(SPECTRAL[t, s]) * fluid[s, :, span]
                    turn = term if turn is None else turn + term
            flux[t, :, span] = total + omega * turn + dfreq * freq[t, :, span]
    for k in range(3):
        acc = None
        for q in range(3):
            term = dot_nt(tags[pl.ds(32 + q * 8, NT), pl.ds(0, L)], stiff[k, q], lax.Precision.HIGHEST)
            acc = term if acc is None else acc + term
        for t in range(NT):
            turn = None
            for s in range(NT):
                term = float(SECOND[t, s]) * tags[pl.ds(32 + k * 8 + s, 1), pl.ds(0, L)]
                turn = term if turn is None else turn + term
            part[k, pl.ds(t, 1), :] = acc[t : t + 1] + omega * omega * tags[pl.ds(8 + k, 1), pl.ds(0, L)] * turn

    points = [
        jnp.concatenate([tags[pl.ds(23 + k, 1), :], tags[pl.ds(26 + k, 1), :]], axis=1)
        for k in range(3)
    ]
    features(points, 1.0, False, feats)
    kept[...] = feats[...]
    cols = feats[...].T.astype(BF16)
    for n, basis in enumerate((basis0, basis1, basis3)):
        if n == 0:
            centres = [tags[pl.ds(2 + k, 1), :] for k in range(3)]
        else:
            ref, at = ((near, 56), (centres3, 0))[n - 1]
            centres = [
                jnp.concatenate(
                    [ref[pl.ds(at + 2 + k, 1), :], ref[pl.ds(at + 10 + k, 1), :]], axis=1
                )
                for k in range(3)
            ]
        basis_of(centres, cols, rows.at[n], squared.at[n], basis)


def edge_kernel(far, jac, tags, out):
    even = (lax.axis_index("cell") & 1) == 0
    at = pl.multiple_of(jnp.where(even, 0, 3 * L), L)
    want = jnp.where(even, 0, 2)
    places = []
    for f in range(NF):
        first, last = tags[pl.ds(11 + f, 1), pl.ds(0, L)], tags[pl.ds(17 + f, 1), pl.ds(L, L)]
        off = jnp.broadcast_to(jnp.where(even, first, last), (8, L)).astype(jnp.int32)
        places.append(iota((8, L), 1) + L + off)
    for t in range(NT):
        sums = [None] * 8
        for f in range(NF):
            got = lanes_of(far[t], places[f] & (L - 1))
            val = jnp.where((places[f] >> 7) == want, got, 0.0)
            gain(sums, jac, f + 1, pl.ds(at, L), val)
        out[t] = fold(sums)


def lookup_kernel(table, tags, other_tags, out, far):
    q = lax.axis_index("sec") & 1
    last = iota((8, L), 0) == 7
    total = table[pl.ds(25, 1), :]
    for p in range(1, CHIPS):
        total = total + table[pl.ds(p * ROWS + 25, 1), :]
    total = jnp.broadcast_to(total, (8, L))
    for other, (tag, to) in enumerate(((tags, out), (other_tags, far))):
        for h in range(2):
            span = pl.ds(h * L, L)
            own = jnp.broadcast_to(tag[pl.ds(0, 1), span], (8, L)).astype(jnp.int32)
            lane = jnp.broadcast_to(tag[pl.ds(1, 1), span], (8, L)).astype(jnp.int32)
            key = jnp.where((own & 1) == q, own >> 1, -1)
            found = [jnp.zeros((8, L), F32) for _ in range(3)]
            for p in range(CHIPS):
                hit = key == p
                for k in range(3):
                    values = table[pl.ds(p * ROWS + k * NT, 8), :]
                    found[k] = jnp.where(hit, lanes_of(values, lane), found[k])
            for k in range(3):
                extra = 0.0 if other else jnp.broadcast_to(tag[pl.ds(2 + k, 1), span], (8, L))
                to[pl.ds(h * 32 + k * 8, 8), :] = jnp.where(last, extra, found[k])
            to[pl.ds(h * 32 + 24, 8), :] = total
    for p in range(CHIPS):
        far[pl.ds(64 + p * 8, 8), :] = table[pl.ds(p * ROWS + 19, 8), :]


def node_sums(table, stride, base, dense):
    q = lax.axis_index("sec") & 1
    block = iota((8, L), 1) >> 4
    for c in range(4):
        shifted = []
        for i in range(8):
            values = table[pl.ds((c * 8 + i) * stride + base, 8), :]
            shifted.append(jnp.where(q == 1, pltpu.roll(values, L - 16, 1), values))
        for g in range(4):
            packed = None
            for i in range(8):
                turn = (16 * i - 32 * g) % L
                moved = pltpu.roll(shifted[i], turn, 1) if turn else shifted[i]
                packed = moved if packed is None else jnp.where(block == i, moved, packed)
            dense[pl.ds(g * 8, 8), pl.ds(c * L, L)] = packed
    tags = dense[pl.ds(29, 1), :].astype(jnp.int32)
    node_hot = jnp.where(iota((L, 512), 0) + 1 == tags, 1.0, 0.0).astype(BF16)
    loads = dot_nt(thirds(dense[...]), node_hot)
    return loads[0:32] + loads[32:64] + loads[64:96]


def own_loads_kernel(table, out, dense):
    out[...] = node_sums(table, ROWS, 19, dense)


def loads_kernel(other, sums, part, out, dense):
    loads = node_sums(other, 8, 64, dense) + sums[...]
    for k, t, size, row in RUNS:
        out[k, pl.ds(t, size), :] = part[k, pl.ds(t, size), :] - loads[row : row + size]


def parts_of(values):
    high = values.astype(BF16).astype(F32)
    rest = values - high
    middle = rest.astype(BF16).astype(F32)
    return high, middle, rest - middle


def features(xyz, scale, ones_first, out):
    at = 0
    square = None
    for point in xyz:
        square = point * point if square is None else square + point * point
        p = [scale * part for part in parts_of(point)]
        order = (0, 0, 1, 1, 0, 2) if ones_first else (0, 1, 0, 1, 2, 0)
        for i in order:
            out[pl.ds(at, 1), :] = p[i]
            at += 1
    one = jnp.ones_like(square)
    squares = list(parts_of(square))
    for row in [one] * 3 + squares if ones_first else squares + [one] * 3:
        out[pl.ds(at, 1), :] = row
        at += 1
    out[pl.ds(24, 8), :] = jnp.zeros((8, square.shape[1]), F32)


def basis_of(centres, cols, rows, squared, basis):
    features(centres, -2.0, True, rows)
    squared[...] = jnp.dot(cols, rows[...].astype(BF16), preferred_element_type=F32)
    for c in range(8):
        span = pl.ds(c * 64, 64)
        gap = jnp.maximum(squared[span, :], 1e-30)
        dist = gap * lax.rsqrt(gap)
        fall = jnp.maximum(1.0 - dist, 0.0)
        fall = fall * fall
        value = fall * fall * (4.0 * dist + 1.0)
        high = value.astype(BF16)
        basis[span, pl.ds(0, 256)] = high
        basis[span, pl.ds(256, 256)] = (value - high.astype(F32)).astype(BF16)


def halves(ref):
    return jnp.concatenate([ref[pl.ds(0, 24), :], ref[pl.ds(32, 24), :]], axis=1)


def moved_by(both, basis):
    high = both.astype(BF16).astype(F32)
    upper = jnp.concatenate([high, both - high], axis=0).astype(BF16)
    lower = jnp.concatenate([high, jnp.zeros_like(high)], axis=0).astype(BF16)
    return dot_nt(basis[...], jnp.concatenate([upper, lower], axis=1))


def own_kernel(d0, kept, basis, out, cols):
    cols[...] = kept[...].T
    out[...] = moved_by(halves(d0), basis)


def block_kernel(ref, cols, moved, out, rows, squared, basis):
    both = halves(ref)
    centres = [both[k * 8 + 7 : k * 8 + 8] for k in range(3)]
    basis_of(centres, cols[...].astype(BF16), rows, squared, basis)
    out[...] = moved[...] + moved_by(both, basis)


def final_kernel(
    d0,
    d1,
    d2,
    d3,
    near_basis,
    third_basis,
    moved,
    sens,
    flux,
    edge,
    struct,
    out,
    struct_out,
    phase_out,
):
    struct_out[...] = struct[...]
    even = (lax.axis_index("cell") & 1) == 0
    span = pl.ds(pl.multiple_of(jnp.where(even, 0, 3 * L), L), L)
    total = moved[...] + moved_by(halves(d3), third_basis) + moved_by(halves(d1), near_basis)
    turned = total.T
    motion = turned[0:24] + turned[24:48]
    for t in range(NT):
        total = flux[t]
        for k in range(3):
            total = total + sens[k] * motion[k * 8 + t : k * 8 + t + 1]
        out[t] = total
        out[t, :, span] = out[t, :, span] + edge[t]
    row = pl.ds(24, 1), pl.ds(0, L)
    total = (d0[row] + d1[row]) + (d2[row] + d3[row])
    total = jnp.where(iota((1, L), 1) >= 96, total, 0.0)
    phase_out[0, 0] = jnp.sum(total)


VM = pl.BlockSpec(memory_space=pltpu.VMEM)
HBM = pl.BlockSpec(memory_space=pltpu.HBM)
SM = pl.BlockSpec(memory_space=pltpu.SMEM)


def kernel(body, name, ins, shapes, outs=None, types=None, scratch=(), size=100000, vmem=32):
    return pl.pallas_call(
        body,
        out_shape=[
            jax.ShapeDtypeStruct(s, t) for s, t in zip(shapes, types or [F32] * len(shapes))
        ],
        in_specs=ins,
        out_specs=outs or [VM] * len(shapes),
        scratch_shapes=list(scratch),
        name=name,
        compiler_params=pltpu.CompilerParams(vmem_limit_bytes=vmem * 1024 * 1024),
        cost_estimate=pl.CostEstimate(flops=1000, bytes_accessed=size, transcendentals=0),
    )


def on_device(
    fluid_delta,
    jacobian,
    face_nbr,
    freq_col,
    grid_sens,
    cell_xyz,
    surf_cell,
    surf_owner,
    surf_node,
    load_proj,
    surf_xyz,
    struct_delta,
    stiffness,
    mass,
    omega,
    freq_delta,
    phase_row,
):
    sections = lax.axis_size("sec")
    columns = lax.axis_size("cell")
    both = sections * columns
    struct = jnp.transpose(struct_delta, (1, 0, 2))
    stiff = jnp.transpose(stiffness, (0, 2, 1, 3))
    jac = jacobian.reshape(NF + 1, 64, 512)
    sens = jnp.transpose(grid_sens, (1, 0, 2))
    owner = surf_owner.reshape(1, 256)
    node = surf_node.reshape(1, 256)
    cell = surf_cell.reshape(1, 256)

    message, tags = kernel(
        prep_kernel,
        "prep",
        [HBM] * 11,
        [(CHIPS * ROWS, L), (56, 256)],
        outs=[HBM, VM],
        scratch=[
            pltpu.VMEM((NT, NV, 512), F32),
            pltpu.VMEM((NT, NV, 512), F32),
            pltpu.VMEM((1, 256), jnp.int32),
            pltpu.VMEM((1, 256), jnp.int32),
            pltpu.VMEM((1, 256), jnp.int32),
            pltpu.VMEM((3, NV, 256), F32),
            pltpu.VMEM((3, NT, L), F32),
            pltpu.VMEM((3, 256), F32),
            pltpu.VMEM((NF, 512), jnp.int32),
            pltpu.VMEM((3, L), F32),
            pltpu.VMEM((3, 512), F32),
            pltpu.VMEM((32, 256), F32),
            pltpu.VMEM((CHIPS * ROWS, L), F32),
            pltpu.SemaphoreType.DMA((11,)),
            pltpu.SemaphoreType.DMA((4,)),
        ],
        vmem=32,
    )(
        *(
            pltpu.with_memory_space_constraint(x, pltpu.HBM)
            for x in (
                fluid_delta,
                phase_row,
                cell,
                owner,
                node,
                load_proj,
                struct,
                surf_xyz,
                face_nbr,
                mass,
                cell_xyz,
            )
        )
    )
    groups = [[2 * i + c for i in range(sections // 2)] for c in range(2)]
    mine = lax.all_to_all(
        message.reshape(CHIPS, 1, ROWS * L), "sec", 0, 0, axis_index_groups=groups, tiled=True
    ).reshape(CHIPS * ROWS, L)
    swap = [(i, i ^ 1) for i in range(sections)]
    other_tags = lax.ppermute(tags, "sec", swap)
    pairs = [[(i, i ^ 1) for i in range(both)], [(i, ((i + 1) ^ 1) - 1) for i in range(1, both - 1)]]
    near_side, far_side, centres = kernel(
        sides_kernel, "sides", [VM] * 2, [(72, L), (NT, NV, L), (16, L)]
    )(fluid_delta, tags)
    centres3 = lax.ppermute(centres, "cell", [(i, i ^ 3) for i in range(columns)])
    near_edge = lax.ppermute(near_side, ("sec", "cell"), pairs[0])
    far_edge = lax.ppermute(far_side, ("sec", "cell"), pairs[1])
    flux, part, kept, *bases = kernel(
        window_kernel,
        "window",
        [VM] * 9,
        [(NT, NV, 512), (3, NT, L), (32, 512)] + [(512, 512)] * 3,
        types=[F32] * 3 + [BF16] * 3,
        scratch=[
            pltpu.VMEM((NF, NT, 8, L), F32),
            pltpu.VMEM((32, 512), F32),
            pltpu.VMEM((3, 32, 256), F32),
            pltpu.VMEM((3, 512, 256), F32),
        ],
        size=4 * 10**6,
    )(
        fluid_delta,
        near_edge,
        centres3,
        jac,
        freq_col,
        stiff,
        tags,
        omega,
        freq_delta,
    )
    mine, flux, far_edge = lax.optimization_barrier((mine, flux, far_edge))
    near, far = kernel(lookup_kernel, "lookup", [VM] * 3, [(64, L), (320, L)])(
        mine, tags, other_tags
    )
    back = lax.ppermute(far, "sec", swap)
    (sums,) = kernel(
        own_loads_kernel, "own_loads", [VM], [(32, L)], scratch=[pltpu.VMEM((32, 512), F32)]
    )(mine)
    (edge,) = kernel(edge_kernel, "edge", [VM] * 3, [(NT, NV, L)])(far_edge, jac, tags)
    back, sums, edge = lax.optimization_barrier((back, sums, edge))
    disp = near + back[:64]
    d2, d3, d1 = (
        lax.ppermute(disp, "cell", [(i, i ^ k) for i in range(columns)]) for k in (2, 3, 1)
    )
    (struct_out,) = kernel(
        loads_kernel,
        "loads",
        [VM] * 3,
        [(3, NT, L)],
        scratch=[pltpu.VMEM((32, 512), F32)],
        size=2 * 10**6,
    )(back, sums, part)
    moved, cols = kernel(own_kernel, "own", [VM] * 3, [(512, 48), (512, 32)])(
        disp, kept, bases[0]
    )
    struct_out, moved, d2 = lax.optimization_barrier((struct_out, moved, d2))
    (moved,) = kernel(
        block_kernel,
        "block",
        [VM] * 3,
        [(512, 48)],
        scratch=[
            pltpu.VMEM((32, 256), F32),
            pltpu.VMEM((512, 256), F32),
            pltpu.VMEM((512, 512), BF16),
        ],
        size=10**6,
    )(d2, cols, moved)
    fluid_out, struct_out, phase_out = kernel(
        final_kernel,
        "final",
        [VM] * 11,
        [(NT, NV, 512), (3, NT, L), (1, 1)],
        outs=[VM, VM, SM],
    )(disp, d1, d2, d3, bases[1], bases[2], moved, sens, flux, edge, struct_out)
    return fluid_out, jnp.transpose(struct_out, (1, 0, 2)), phase_out.reshape(1)


def solution(mesh):
    split = ("sec", "cell")
    return jax.shard_map(
        on_device,
        mesh=mesh,
        in_specs=(
            P(None, None, split),
            P(None, None, None, split),
            P(None, split),
            P(None, None, split),
            P(None, None, split),
            P(None, split),
            P(split),
            P(split, None),
            P(split),
            P(None, None, split),
            P(None, split),
            P(None, None, split),
            P(None, None, None, split),
            P(None, split),
            P(),
            P(),
            P(None, None, split),
        ),
        out_specs=(P(None, None, split), P(None, None, split), P()),
        check_vma=False,
    )
```

```python
import functools

import jax
import jax.numpy as jnp
import numpy as np
from jax import lax
from jax.experimental import pallas as pl
from jax.experimental.pallas import tpu as pltpu
from jax.sharding import PartitionSpec as P

NT = 7
NV = 8
NF = 6
L = 128
CHIPS = 32
CAP = 16
ROWS = 27
RUNS = ((0, 0, 6, 2), (0, 6, 1, 10), (1, 0, 5, 11), (1, 5, 2, 18), (2, 0, 4, 20), (2, 4, 3, 26))
F32 = jnp.float32
BF16 = jnp.bfloat16


def spectral_table(instances):
    positions = np.arange(instances)
    offset = positions[:, None] - positions[None, :]
    clipped = np.where(offset == 0, 1, offset)
    return np.where(
        offset == 0, 0.0, 0.5 * (-1.0) ** offset / np.sin(np.pi * clipped / instances)
    )


SPECTRAL = np.asarray(spectral_table(NT), np.float32)
SECOND = np.asarray(spectral_table(NT) @ spectral_table(NT), np.float32)


def iota(shape, axis):
    return lax.broadcasted_iota(jnp.int32, shape, axis)


def lanes_of(values, index):
    return jnp.take_along_axis(values, index, axis=1, mode="promise_in_bounds")


def thirds(values):
    high = values.astype(BF16)
    rest = values - high.astype(F32)
    middle = rest.astype(BF16)
    low = (rest - middle.astype(F32)).astype(BF16)
    return jnp.concatenate([high, middle, low], axis=0)


def dot_nt(a, b, precision=None):
    return lax.dot_general(
        a, b, (((1,), (1,)), ((), ())), precision=precision, preferred_element_type=F32
    )


def prep_kernel(*refs):
    far, out, tags, near = refs[:11], refs[11], refs[12], refs[13:24]
    pay, message, sems, out_sems = refs[24:]
    tag_rows, sent = tags, []
    fluid, phase, cell, owner, node, proj, struct, xyz, nbr, mass, cells = near
    copies = [pltpu.make_async_copy(a, b, sems.at[i]) for i, (a, b) in enumerate(zip(far, near))]
    for i in (3, 4, 2, 0, 5, 6, 7, 8, 9, 10, 1):
        copies[i].start()
    pay[...] = jnp.zeros_like(pay)
    copies[3].wait()
    own = owner[...]
    hot = jnp.where(iota((64, 256), 0) == own, 1.0, 0.0)
    before = jnp.where(iota((256, 256), 0) < iota((256, 256), 1), 1.0, 0.0).astype(BF16)
    counts = jnp.dot(hot.astype(BF16), before, preferred_element_type=F32)
    rank = jnp.sum(hot * counts, axis=0, keepdims=True)
    slot = own * CAP + rank.astype(jnp.int32)
    slot_hot = jnp.where(iota((1024, 256), 0) == slot, 1.0, 0.0).astype(BF16)
    copies[4].wait()
    pay[pl.ds(27, 1), :] = (node[...] + 1).astype(F32)
    copies[2].wait()
    copies[6].wait()
    for p in range(CHIPS):
        for k in range(3):
            message[pl.ds(p * ROWS + k * NT, NT), :] = struct[k]
    copies[0].wait()
    copies[5].wait()
    for i in range(7, 11):
        copies[i].wait()
    tag_rows[...] = jnp.zeros_like(tag_rows)
    tag_rows[pl.ds(0, 1), :] = own.astype(F32)
    tag_rows[pl.ds(1, 1), :] = node[...].astype(F32)
    tag_rows[pl.ds(2, 3), :] = xyz[...]
    for k in range(3):
        tag_rows[pl.ds(32 + k * 8, NT), pl.ds(0, L)] = struct[k]
    tag_rows[pl.ds(8, 3), pl.ds(0, L)] = mass[...]
    for h in range(2):
        half = pl.ds(h * 256, 256)
        tag_rows[pl.ds(11 + 6 * h, 6), :] = nbr[:, half].astype(F32)
        tag_rows[pl.ds(23 + 3 * h, 3), :] = cells[:, half]
    for h in range(2):
        span = pl.ds(h * L, L)
        index = jnp.broadcast_to(cell[:, span], (8, L))
        lane, chunk = index & (L - 1), index >> 7
        for t in range(NT):
            got = lanes_of(fluid[t, :, pl.ds(0, L)], lane)
            for c in range(1, 4):
                got = jnp.where(chunk == c, lanes_of(fluid[t, :, pl.ds(c * L, L)], lane), got)
            for k in range(3):
                f = k * NT + t
                row = f // 6 * 8 + f % 6
                pay[pl.ds(row, 1), span] = jnp.sum(proj[k, :, span] * got, axis=0, keepdims=True)
    slotted = dot_nt(thirds(pay[...]), slot_hot)
    slotted = slotted[0:32] + slotted[32:64] + slotted[64:96]

    copies[1].wait()
    part = phase[0] * fluid[0]
    for t in range(1, NT):
        part = part + phase[t] * fluid[t]
    part = jnp.sum(part, axis=0, keepdims=True)
    part = part[:, 0:L] + part[:, L : 2 * L] + part[:, 2 * L : 3 * L] + part[:, 3 * L : 4 * L]
    part = part + pltpu.roll(part, 64, 1)
    part = part + pltpu.roll(part, 32, 1)
    is_phase = iota((8, L), 0) == 4
    place = iota((8, L), 1) >> 5
    for c in range(8):
        groups = [slotted[g * 8 : g * 8 + 8, c * L : c * L + L] for g in range(4)]
        groups[3] = jnp.where(is_phase, part, groups[3])
        turned = []
        for d in range(4):
            mixed = groups[d]
            for j in range(1, 4):
                mixed = jnp.where(place == j, groups[(j + d) % 4], mixed)
            turned.append(pltpu.roll(mixed, 32 * d, 1) if d else mixed)
        for j in range(4):
            packed = turned[(0 - j) % 4]
            for g in range(1, 4):
                packed = jnp.where(place == g, turned[(g - j) % 4], packed)
            message[pl.ds((c * 4 + j) * ROWS + 21, 6), :] = packed[0:6]
        if c % 2:
            span = pl.ds((c - 1) * 4 * ROWS, 8 * ROWS)
            copy = pltpu.make_async_copy(message.at[span], out.at[span], out_sems.at[c // 2])
            copy.start()
            sent.append(copy)
    for copy in sent:
        copy.wait()


def sides_kernel(fluid, tags, near, far, centres):
    even = (lax.axis_index("cell") & 1) == 0
    for t in range(NT):
        first, last = fluid[t, :, pl.ds(0, L)], fluid[t, :, pl.ds(3 * L, L)]
        near[pl.ds(t * 8, 8), :] = jnp.where(even, last, first)
        far[t] = jnp.where(even, first, last)
    for h in range(2):
        near[pl.ds(56 + 8 * h, 8), :] = tags[pl.ds(0, 8), pl.ds(h * L, L)]
        centres[pl.ds(8 * h, 8), :] = tags[pl.ds(0, 8), pl.ds(h * L, L)]


def fold(level):
    for s in (4, 2, 1):
        half = len(level) // 2
        low = (iota((8, L), 0) & s) == 0
        level = [
            jnp.where(
                low,
                level[v] + pltpu.roll(level[v], 8 - s, 0),
                level[v + half] + pltpu.roll(level[v + half], s, 0),
            )
            for v in range(half)
        ]
    return level[0]


def gain(sums, jac, f, span, val):
    for vv in range(4):
        pair = jac[f, pl.ds(vv * 16, 16), span].astype(F32)
        for u in range(2):
            term = pair[u * 8 : u * 8 + 8] * val
            v = vv * 2 + u
            sums[v] = term if sums[v] is None else sums[v] + term


def window_kernel(
    fluid,
    near,
    centres3,
    jac,
    freq,
    stiff,
    tags,
    omega_ref,
    dfreq_ref,
    flux,
    part,
    kept,
    basis0,
    basis1,
    basis3,
    gathered,
    feats,
    rows,
    squared,
):
    even = (lax.axis_index("cell") & 1) == 0
    omega = omega_ref[...].reshape(1, 1)
    dfreq = dfreq_ref[...].reshape(1, 1)
    for i in range(4):
        span = pl.ds(i * L, L)
        for f in range(NF):
            row = tags[pl.ds(11 + 6 * (i // 2) + f, 1), pl.ds(i % 2 * L, L)]
            off = jnp.broadcast_to(row, (8, L)).astype(jnp.int32)
            place = iota((8, L), 1) + L + off
            lane = place & (L - 1)
            which = jnp.where(off == 0, 3, place >> 7)
            for t in range(NT):
                got = jnp.zeros((8, L), F32)
                for q in range(3):
                    j = i + q
                    if j in (0, 5):
                        src = jnp.where(even == (j == 5), near[pl.ds(t * 8, 8), :], 0.0)
                    else:
                        src = fluid[t, :, pl.ds((j - 1) * L, L)]
                    got = jnp.where(which == q, lanes_of(src, lane), got)
                gathered[f, t] = got
        for t in range(NT):
            here = fluid[t, :, span]
            sums = [None] * 8
            for f in range(NF + 1):
                val = here if f == 0 else gathered[f - 1, t]
                gain(sums, jac, f, span, val)
            total = fold(sums)
            turn = None
            for s in range(NT):
                if s != t:
                    term = float(SPECTRAL[t, s]) * fluid[s, :, span]
                    turn = term if turn is None else turn + term
            flux[t, :, span] = total + omega * turn + dfreq * freq[t, :, span]
    for k in range(3):
        acc = None
        for q in range(3):
            term = dot_nt(tags[pl.ds(32 + q * 8, NT), pl.ds(0, L)], stiff[k, q], lax.Precision.HIGHEST)
            acc = term if acc is None else acc + term
        for t in range(NT):
            turn = None
            for s in range(NT):
                term = float(SECOND[t, s]) * tags[pl.ds(32 + k * 8 + s, 1), pl.ds(0, L)]
                turn = term if turn is None else turn + term
            part[k, pl.ds(t, 1), :] = acc[t : t + 1] + omega * omega * tags[pl.ds(8 + k, 1), pl.ds(0, L)] * turn

    points = [
        jnp.concatenate([tags[pl.ds(23 + k, 1), :], tags[pl.ds(26 + k, 1), :]], axis=1)
        for k in range(3)
    ]
    features(points, 1.0, False, feats)
    kept[...] = feats[...]
    cols = feats[...].T.astype(BF16)
    for n, basis in enumerate((basis0, basis1, basis3)):
        if n == 0:
            centres = [tags[pl.ds(2 + k, 1), :] for k in range(3)]
        else:
            ref, at = ((near, 56), (centres3, 0))[n - 1]
            centres = [
                jnp.concatenate(
                    [ref[pl.ds(at + 2 + k, 1), :], ref[pl.ds(at + 10 + k, 1), :]], axis=1
                )
                for k in range(3)
            ]
        basis_of(centres, cols, rows.at[n], squared.at[n], basis)


def edge_kernel(far, jac, tags, out):
    even = (lax.axis_index("cell") & 1) == 0
    at = pl.multiple_of(jnp.where(even, 0, 3 * L), L)
    want = jnp.where(even, 0, 2)
    places = []
    for f in range(NF):
        first, last = tags[pl.ds(11 + f, 1), pl.ds(0, L)], tags[pl.ds(17 + f, 1), pl.ds(L, L)]
        off = jnp.broadcast_to(jnp.where(even, first, last), (8, L)).astype(jnp.int32)
        places.append(iota((8, L), 1) + L + off)
    for t in range(NT):
        sums = [None] * 8
        for f in range(NF):
            got = lanes_of(far[t], places[f] & (L - 1))
            val = jnp.where((places[f] >> 7) == want, got, 0.0)
            gain(sums, jac, f + 1, pl.ds(at, L), val)
        out[t] = fold(sums)


def answer(table, tag, out, own):
    q = lax.axis_index("sec") & 1
    last = iota((8, L), 0) == 7
    total = table[pl.ds(25, 1), :]
    for p in range(1, CHIPS):
        total = total + table[pl.ds(p * ROWS + 25, 1), :]
    total = jnp.broadcast_to(total, (8, L))
    for h in range(2):
        span = pl.ds(h * L, L)
        owner = jnp.broadcast_to(tag[pl.ds(0, 1), span], (8, L)).astype(jnp.int32)
        lane = jnp.broadcast_to(tag[pl.ds(1, 1), span], (8, L)).astype(jnp.int32)
        key = jnp.where((owner & 1) == q, owner >> 1, -1)
        found = [jnp.zeros((8, L), F32) for _ in range(3)]
        for p in range(CHIPS):
            hit = key == p
            for k in range(3):
                values = table[pl.ds(p * ROWS + k * NT, 8), :]
                found[k] = jnp.where(hit, lanes_of(values, lane), found[k])
        for k in range(3):
            extra = jnp.broadcast_to(tag[pl.ds(2 + k, 1), span], (8, L)) if own else 0.0
            out[pl.ds(h * 32 + k * 8, 8), :] = jnp.where(last, extra, found[k])
        out[pl.ds(h * 32 + 24, 8), :] = total


def near_kernel(table, tags, out):
    answer(table, tags, out, True)


def far_kernel(table, other_tags, out):
    answer(table, other_tags, out, False)
    q = lax.axis_index("sec") & 1
    block = (iota((8, L), 1) >> 4) & 1
    for p in range(CHIPS // 2):
        first = table[pl.ds(2 * p * ROWS + 19, 8), :]
        second = table[pl.ds((2 * p + 1) * ROWS + 19, 8), :]
        first = jnp.where(q == 0, pltpu.roll(first, L - 16, 1), first)
        second = jnp.where(q == 0, second, pltpu.roll(second, 16, 1))
        out[pl.ds(64 + p * 8, 8), :] = jnp.where(block == 0, first, second)


def node_sums(source, dense):
    block = iota((8, L), 1) >> 4
    for c in range(4):
        shifted = [source(c * 8 + i) for i in range(8)]
        for g in range(4):
            packed = None
            for i in range(8):
                turn = (16 * i - 32 * g) % L
                moved = pltpu.roll(shifted[i], turn, 1) if turn else shifted[i]
                packed = moved if packed is None else jnp.where(block == i, moved, packed)
            dense[pl.ds(g * 8, 8), pl.ds(c * L, L)] = packed
    tags = dense[pl.ds(29, 1), :].astype(jnp.int32)
    node_hot = jnp.where(iota((L, 512), 0) + 1 == tags, 1.0, 0.0).astype(BF16)
    loads = dot_nt(thirds(dense[...]), node_hot)
    return loads[0:32] + loads[32:64] + loads[64:96]


def own_loads_kernel(table, out, dense):
    q = lax.axis_index("sec") & 1

    def source(p):
        values = table[pl.ds(p * ROWS + 19, 8), :]
        return jnp.where(q == 1, pltpu.roll(values, L - 16, 1), values)

    out[...] = node_sums(source, dense)


def loads_kernel(other, sums, part, out, dense):
    def source(p):
        values = other[pl.ds(64 + p // 2 * 8, 8), :]
        return pltpu.roll(values, L - 16, 1) if p % 2 else values

    loads = node_sums(source, dense) + sums[...]
    for k, t, size, row in RUNS:
        out[k, pl.ds(t, size), :] = part[k, pl.ds(t, size), :] - loads[row : row + size]


def parts_of(values):
    high = values.astype(BF16).astype(F32)
    rest = values - high
    middle = rest.astype(BF16).astype(F32)
    return high, middle, rest - middle


def features(xyz, scale, ones_first, out):
    at = 0
    square = None
    for point in xyz:
        square = point * point if square is None else square + point * point
        p = [scale * part for part in parts_of(point)]
        order = (0, 0, 1, 1, 0, 2) if ones_first else (0, 1, 0, 1, 2, 0)
        for i in order:
            out[pl.ds(at, 1), :] = p[i]
            at += 1
    one = jnp.ones_like(square)
    squares = list(parts_of(square))
    for row in [one] * 3 + squares if ones_first else squares + [one] * 3:
        out[pl.ds(at, 1), :] = row
        at += 1
    out[pl.ds(24, 8), :] = jnp.zeros((8, square.shape[1]), F32)


def basis_of(centres, cols, rows, squared, basis):
    features(centres, -2.0, True, rows)
    squared[...] = jnp.dot(cols, rows[...].astype(BF16), preferred_element_type=F32)
    for c in range(8):
        span = pl.ds(c * 64, 64)
        gap = jnp.maximum(squared[span, :], 1e-30)
        dist = gap * lax.rsqrt(gap)
        fall = jnp.maximum(1.0 - dist, 0.0)
        fall = fall * fall
        value = fall * fall * (4.0 * dist + 1.0)
        high = value.astype(BF16)
        basis[span, pl.ds(0, 256)] = high
        basis[span, pl.ds(256, 256)] = (value - high.astype(F32)).astype(BF16)


def halves(ref):
    return jnp.concatenate([ref[pl.ds(0, 24), :], ref[pl.ds(32, 24), :]], axis=1)


def moved_by(both, basis):
    high = both.astype(BF16).astype(F32)
    upper = jnp.concatenate([high, both - high], axis=0).astype(BF16)
    lower = jnp.concatenate([high, jnp.zeros_like(high)], axis=0).astype(BF16)
    return dot_nt(basis[...], jnp.concatenate([upper, lower], axis=1))


def own_kernel(d0, kept, basis, out, cols):
    cols[...] = kept[...].T
    out[...] = moved_by(halves(d0), basis)


def block_kernel(ref, cols, moved, out, rows, squared, basis):
    both = halves(ref)
    centres = [both[k * 8 + 7 : k * 8 + 8] for k in range(3)]
    basis_of(centres, cols[...].astype(BF16), rows, squared, basis)
    out[...] = moved[...] + moved_by(both, basis)


def final_kernel(
    d0,
    d1,
    d2,
    d3,
    near_basis,
    third_basis,
    moved,
    sens,
    flux,
    edge,
    struct,
    out,
    struct_out,
    phase_out,
):
    struct_out[...] = struct[...]
    even = (lax.axis_index("cell") & 1) == 0
    span = pl.ds(pl.multiple_of(jnp.where(even, 0, 3 * L), L), L)
    total = moved[...] + moved_by(halves(d3), third_basis) + moved_by(halves(d1), near_basis)
    turned = total.T
    motion = turned[0:24] + turned[24:48]
    for t in range(NT):
        total = flux[t]
        for k in range(3):
            total = total + sens[k] * motion[k * 8 + t : k * 8 + t + 1]
        out[t] = total
        out[t, :, span] = out[t, :, span] + edge[t]
    row = pl.ds(24, 1), pl.ds(0, L)
    total = (d0[row] + d1[row]) + (d2[row] + d3[row])
    total = jnp.where(iota((1, L), 1) >= 96, total, 0.0)
    phase_out[0, 0] = jnp.sum(total)


VM = pl.BlockSpec(memory_space=pltpu.VMEM)
HBM = pl.BlockSpec(memory_space=pltpu.HBM)
SM = pl.BlockSpec(memory_space=pltpu.SMEM)


def kernel(body, name, ins, shapes, outs=None, types=None, scratch=(), size=100000, vmem=32):
    return pl.pallas_call(
        body,
        out_shape=[
            jax.ShapeDtypeStruct(s, t) for s, t in zip(shapes, types or [F32] * len(shapes))
        ],
        in_specs=ins,
        out_specs=outs or [VM] * len(shapes),
        scratch_shapes=list(scratch),
        name=name,
        compiler_params=pltpu.CompilerParams(vmem_limit_bytes=vmem * 1024 * 1024),
        cost_estimate=pl.CostEstimate(flops=1000, bytes_accessed=size, transcendentals=0),
    )


def on_device(
    fluid_delta,
    jacobian,
    face_nbr,
    freq_col,
    grid_sens,
    cell_xyz,
    surf_cell,
    surf_owner,
    surf_node,
    load_proj,
    surf_xyz,
    struct_delta,
    stiffness,
    mass,
    omega,
    freq_delta,
    phase_row,
):
    sections = lax.axis_size("sec")
    columns = lax.axis_size("cell")
    both = sections * columns
    struct = jnp.transpose(struct_delta, (1, 0, 2))
    stiff = jnp.transpose(stiffness, (0, 2, 1, 3))
    jac = jacobian.reshape(NF + 1, 64, 512)
    sens = jnp.transpose(grid_sens, (1, 0, 2))
    owner = surf_owner.reshape(1, 256)
    node = surf_node.reshape(1, 256)
    cell = surf_cell.reshape(1, 256)

    message, tags = kernel(
        prep_kernel,
        "prep",
        [HBM] * 11,
        [(CHIPS * ROWS, L), (56, 256)],
        outs=[HBM, VM],
        scratch=[
            pltpu.VMEM((NT, NV, 512), F32),
            pltpu.VMEM((NT, NV, 512), F32),
            pltpu.VMEM((1, 256), jnp.int32),
            pltpu.VMEM((1, 256), jnp.int32),
            pltpu.VMEM((1, 256), jnp.int32),
            pltpu.VMEM((3, NV, 256), F32),
            pltpu.VMEM((3, NT, L), F32),
            pltpu.VMEM((3, 256), F32),
            pltpu.VMEM((NF, 512), jnp.int32),
            pltpu.VMEM((3, L), F32),
            pltpu.VMEM((3, 512), F32),
            pltpu.VMEM((32, 256), F32),
            pltpu.VMEM((CHIPS * ROWS, L), F32),
            pltpu.SemaphoreType.DMA((11,)),
            pltpu.SemaphoreType.DMA((4,)),
        ],
        vmem=32,
    )(
        *(
            pltpu.with_memory_space_constraint(x, pltpu.HBM)
            for x in (
                fluid_delta,
                phase_row,
                cell,
                owner,
                node,
                load_proj,
                struct,
                surf_xyz,
                face_nbr,
                mass,
                cell_xyz,
            )
        )
    )
    groups = [[2 * i + c for i in range(sections // 2)] for c in range(2)]
    mine = lax.all_to_all(
        message.reshape(CHIPS, 1, ROWS * L), "sec", 0, 0, axis_index_groups=groups, tiled=True
    ).reshape(CHIPS * ROWS, L)
    swap = [(i, i ^ 1) for i in range(sections)]
    other_tags = lax.ppermute(tags, "sec", swap)
    pairs = [[(i, i ^ 1) for i in range(both)], [(i, ((i + 1) ^ 1) - 1) for i in range(1, both - 1)]]
    near_side, far_side, centres = kernel(
        sides_kernel, "sides", [VM] * 2, [(72, L), (NT, NV, L), (16, L)]
    )(fluid_delta, tags)
    centres3 = lax.ppermute(centres, "cell", [(i, i ^ 3) for i in range(columns)])
    near_edge = lax.ppermute(near_side, ("sec", "cell"), pairs[0])
    far_edge = lax.ppermute(far_side, ("sec", "cell"), pairs[1])
    flux, part, kept, *bases = kernel(
        window_kernel,
        "window",
        [VM] * 9,
        [(NT, NV, 512), (3, NT, L), (32, 512)] + [(512, 512)] * 3,
        types=[F32] * 3 + [BF16] * 3,
        scratch=[
            pltpu.VMEM((NF, NT, 8, L), F32),
            pltpu.VMEM((32, 512), F32),
            pltpu.VMEM((3, 32, 256), F32),
            pltpu.VMEM((3, 512, 256), F32),
        ],
        size=4 * 10**6,
    )(
        fluid_delta,
        near_edge,
        centres3,
        jac,
        freq_col,
        stiff,
        tags,
        omega,
        freq_delta,
    )
    mine, flux, far_edge = lax.optimization_barrier((mine, flux, far_edge))
    (far,) = kernel(far_kernel, "far", [VM] * 2, [(192, L)])(mine, other_tags)
    back = lax.ppermute(far, "sec", swap)
    (near,) = kernel(near_kernel, "near", [VM] * 2, [(64, L)])(mine, tags)
    (sums,) = kernel(
        own_loads_kernel, "own_loads", [VM], [(32, L)], scratch=[pltpu.VMEM((32, 512), F32)]
    )(mine)
    back, near, sums = lax.optimization_barrier((back, near, sums))
    disp = near + back[:64]
    d2, d3, d1 = (
        lax.ppermute(disp, "cell", [(i, i ^ k) for i in range(columns)]) for k in (2, 3, 1)
    )
    (struct_out,) = kernel(
        loads_kernel,
        "loads",
        [VM] * 3,
        [(3, NT, L)],
        scratch=[pltpu.VMEM((32, 512), F32)],
        size=2 * 10**6,
    )(back, sums, part)
    moved, cols = kernel(own_kernel, "own", [VM] * 3, [(512, 48), (512, 32)])(
        disp, kept, bases[0]
    )
    (edge,) = kernel(edge_kernel, "edge", [VM] * 3, [(NT, NV, L)])(far_edge, jac, tags)
    struct_out, moved, edge, d2 = lax.optimization_barrier((struct_out, moved, edge, d2))
    (moved,) = kernel(
        block_kernel,
        "block",
        [VM] * 3,
        [(512, 48)],
        scratch=[
            pltpu.VMEM((32, 256), F32),
            pltpu.VMEM((512, 256), F32),
            pltpu.VMEM((512, 512), BF16),
        ],
        size=10**6,
    )(d2, cols, moved)
    fluid_out, struct_out, phase_out = kernel(
        final_kernel,
        "final",
        [VM] * 11,
        [(NT, NV, 512), (3, NT, L), (1, 1)],
        outs=[VM, VM, SM],
    )(disp, d1, d2, d3, bases[1], bases[2], moved, sens, flux, edge, struct_out)
    return fluid_out, jnp.transpose(struct_out, (1, 0, 2)), phase_out.reshape(1)


def solution(mesh):
    split = ("sec", "cell")
    return jax.shard_map(
        on_device,
        mesh=mesh,
        in_specs=(
            P(None, None, split),
            P(None, None, None, split),
            P(None, split),
            P(None, None, split),
            P(None, None, split),
            P(None, split),
            P(split),
            P(split, None),
            P(split),
            P(None, None, split),
            P(None, split),
            P(None, None, split),
            P(None, None, None, split),
            P(None, split),
            P(),
            P(),
            P(None, None, split),
        ),
        out_specs=(P(None, None, split), P(None, None, split), P()),
        check_vma=False,
    )
```

```python
import functools

import jax
import jax.numpy as jnp
import numpy as np
from jax import lax
from jax.experimental import pallas as pl
from jax.experimental.pallas import tpu as pltpu
from jax.sharding import PartitionSpec as P

NT = 7
NV = 8
NF = 6
L = 128
CHIPS = 32
CAP = 16
ROWS = 27
RUNS = ((0, 0, 6, 2), (0, 6, 1, 10), (1, 0, 5, 11), (1, 5, 2, 18), (2, 0, 4, 20), (2, 4, 3, 26))
F32 = jnp.float32
BF16 = jnp.bfloat16


def spectral_table(instances):
    positions = np.arange(instances)
    offset = positions[:, None] - positions[None, :]
    clipped = np.where(offset == 0, 1, offset)
    return np.where(
        offset == 0, 0.0, 0.5 * (-1.0) ** offset / np.sin(np.pi * clipped / instances)
    )


SPECTRAL = np.asarray(spectral_table(NT), np.float32)
SECOND = np.asarray(spectral_table(NT) @ spectral_table(NT), np.float32)


def iota(shape, axis):
    return lax.broadcasted_iota(jnp.int32, shape, axis)


def lanes_of(values, index):
    return jnp.take_along_axis(values, index, axis=1, mode="promise_in_bounds")


def thirds(values):
    high = values.astype(BF16)
    rest = values - high.astype(F32)
    middle = rest.astype(BF16)
    low = (rest - middle.astype(F32)).astype(BF16)
    return jnp.concatenate([high, middle, low], axis=0)


def dot_nt(a, b, precision=None):
    return lax.dot_general(
        a, b, (((1,), (1,)), ((), ())), precision=precision, preferred_element_type=F32
    )


def prep_kernel(*refs):
    far, out, tags, near = refs[:11], refs[11], refs[12], refs[13:24]
    pay, message, sems, out_sems = refs[24:]
    tag_rows, sent = tags, []
    fluid, phase, cell, owner, node, proj, struct, xyz, nbr, mass, cells = near
    copies = [pltpu.make_async_copy(a, b, sems.at[i]) for i, (a, b) in enumerate(zip(far, near))]
    for i in (3, 4, 2, 0, 5, 6, 7, 8, 9, 10, 1):
        copies[i].start()
    pay[...] = jnp.zeros_like(pay)
    copies[3].wait()
    own = owner[...]
    hot = jnp.where(iota((64, 256), 0) == own, 1.0, 0.0)
    before = jnp.where(iota((256, 256), 0) < iota((256, 256), 1), 1.0, 0.0).astype(BF16)
    counts = jnp.dot(hot.astype(BF16), before, preferred_element_type=F32)
    rank = jnp.sum(hot * counts, axis=0, keepdims=True)
    slot = own * CAP + rank.astype(jnp.int32)
    slot_hot = jnp.where(iota((1024, 256), 0) == slot, 1.0, 0.0).astype(BF16)
    copies[4].wait()
    pay[pl.ds(27, 1), :] = (node[...] + 1).astype(F32)
    copies[2].wait()
    copies[6].wait()
    for p in range(CHIPS):
        for k in range(3):
            message[pl.ds(p * ROWS + k * NT, NT), :] = struct[k]
    copies[0].wait()
    copies[5].wait()
    for i in range(7, 11):
        copies[i].wait()
    tag_rows[...] = jnp.zeros_like(tag_rows)
    tag_rows[pl.ds(0, 1), :] = own.astype(F32)
    tag_rows[pl.ds(1, 1), :] = node[...].astype(F32)
    tag_rows[pl.ds(2, 3), :] = xyz[...]
    for k in range(3):
        tag_rows[pl.ds(32 + k * 8, NT), pl.ds(0, L)] = struct[k]
    tag_rows[pl.ds(8, 3), pl.ds(0, L)] = mass[...]
    for h in range(2):
        half = pl.ds(h * 256, 256)
        tag_rows[pl.ds(11 + 6 * h, 6), :] = nbr[:, half].astype(F32)
        tag_rows[pl.ds(23 + 3 * h, 3), :] = cells[:, half]
    for h in range(2):
        span = pl.ds(h * L, L)
        index = jnp.broadcast_to(cell[:, span], (8, L))
        lane, chunk = index & (L - 1), index >> 7
        for t in range(NT):
            got = lanes_of(fluid[t, :, pl.ds(0, L)], lane)
            for c in range(1, 4):
                got = jnp.where(chunk == c, lanes_of(fluid[t, :, pl.ds(c * L, L)], lane), got)
            for k in range(3):
                f = k * NT + t
                row = f // 6 * 8 + f % 6
                pay[pl.ds(row, 1), span] = jnp.sum(proj[k, :, span] * got, axis=0, keepdims=True)
    slotted = dot_nt(thirds(pay[...]), slot_hot)
    slotted = slotted[0:32] + slotted[32:64] + slotted[64:96]

    copies[1].wait()
    part = phase[0] * fluid[0]
    for t in range(1, NT):
        part = part + phase[t] * fluid[t]
    part = jnp.sum(part, axis=0, keepdims=True)
    part = part[:, 0:L] + part[:, L : 2 * L] + part[:, 2 * L : 3 * L] + part[:, 3 * L : 4 * L]
    part = part + pltpu.roll(part, 64, 1)
    part = part + pltpu.roll(part, 32, 1)
    is_phase = iota((8, L), 0) == 4
    place = iota((8, L), 1) >> 5
    for c in range(8):
        groups = [slotted[g * 8 : g * 8 + 8, c * L : c * L + L] for g in range(4)]
        groups[3] = jnp.where(is_phase, part, groups[3])
        turned = []
        for d in range(4):
            mixed = groups[d]
            for j in range(1, 4):
                mixed = jnp.where(place == j, groups[(j + d) % 4], mixed)
            turned.append(pltpu.roll(mixed, 32 * d, 1) if d else mixed)
        for j in range(4):
            packed = turned[(0 - j) % 4]
            for g in range(1, 4):
                packed = jnp.where(place == g, turned[(g - j) % 4], packed)
            message[pl.ds((c * 4 + j) * ROWS + 21, 6), :] = packed[0:6]
        if c % 2:
            span = pl.ds((c - 1) * 4 * ROWS, 8 * ROWS)
            copy = pltpu.make_async_copy(message.at[span], out.at[span], out_sems.at[c // 2])
            copy.start()
            sent.append(copy)
    for copy in sent:
        copy.wait()


def sides_kernel(fluid, tags, near, far, centres):
    even = (lax.axis_index("cell") & 1) == 0
    for t in range(NT):
        first, last = fluid[t, :, pl.ds(0, L)], fluid[t, :, pl.ds(3 * L, L)]
        near[pl.ds(t * 8, 8), :] = jnp.where(even, last, first)
        far[t] = jnp.where(even, first, last)
    for h in range(2):
        near[pl.ds(56 + 8 * h, 8), :] = tags[pl.ds(0, 8), pl.ds(h * L, L)]
        centres[pl.ds(8 * h, 8), :] = tags[pl.ds(0, 8), pl.ds(h * L, L)]


def fold(level):
    for s in (4, 2, 1):
        half = len(level) // 2
        low = (iota((8, L), 0) & s) == 0
        level = [
            jnp.where(
                low,
                level[v] + pltpu.roll(level[v], 8 - s, 0),
                level[v + half] + pltpu.roll(level[v + half], s, 0),
            )
            for v in range(half)
        ]
    return level[0]


def gain(sums, jac, f, span, val):
    for vv in range(4):
        pair = jac[f, pl.ds(vv * 16, 16), span].astype(F32)
        for u in range(2):
            term = pair[u * 8 : u * 8 + 8] * val
            v = vv * 2 + u
            sums[v] = term if sums[v] is None else sums[v] + term


def window_kernel(
    fluid,
    near,
    centres3,
    jac,
    freq,
    stiff,
    tags,
    omega_ref,
    dfreq_ref,
    flux,
    part,
    kept,
    basis0,
    basis1,
    basis3,
    gathered,
    feats,
    rows,
    squared,
):
    even = (lax.axis_index("cell") & 1) == 0
    omega = omega_ref[...].reshape(1, 1)
    dfreq = dfreq_ref[...].reshape(1, 1)
    for i in range(4):
        span = pl.ds(i * L, L)
        for f in range(NF):
            row = tags[pl.ds(11 + 6 * (i // 2) + f, 1), pl.ds(i % 2 * L, L)]
            off = jnp.broadcast_to(row, (8, L)).astype(jnp.int32)
            place = iota((8, L), 1) + L + off
            lane = place & (L - 1)
            which = jnp.where(off == 0, 3, place >> 7)
            for t in range(NT):
                got = jnp.zeros((8, L), F32)
                for q in range(3):
                    j = i + q
                    if j in (0, 5):
                        src = jnp.where(even == (j == 5), near[pl.ds(t * 8, 8), :], 0.0)
                    else:
                        src = fluid[t, :, pl.ds((j - 1) * L, L)]
                    got = jnp.where(which == q, lanes_of(src, lane), got)
                gathered[f, t] = got
        for t in range(NT):
            here = fluid[t, :, span]
            sums = [None] * 8
            for f in range(NF + 1):
                val = here if f == 0 else gathered[f - 1, t]
                gain(sums, jac, f, span, val)
            total = fold(sums)
            turn = None
            for s in range(NT):
                if s != t:
                    term = float(SPECTRAL[t, s]) * fluid[s, :, span]
                    turn = term if turn is None else turn + term
            flux[t, :, span] = total + omega * turn + dfreq * freq[t, :, span]
    for k in range(3):
        acc = None
        for q in range(3):
            term = dot_nt(tags[pl.ds(32 + q * 8, NT), pl.ds(0, L)], stiff[k, q], lax.Precision.HIGHEST)
            acc = term if acc is None else acc + term
        for t in range(NT):
            turn = None
            for s in range(NT):
                term = float(SECOND[t, s]) * tags[pl.ds(32 + k * 8 + s, 1), pl.ds(0, L)]
                turn = term if turn is None else turn + term
            part[k, pl.ds(t, 1), :] = acc[t : t + 1] + omega * omega * tags[pl.ds(8 + k, 1), pl.ds(0, L)] * turn

    points = [
        jnp.concatenate([tags[pl.ds(23 + k, 1), :], tags[pl.ds(26 + k, 1), :]], axis=1)
        for k in range(3)
    ]
    features(points, 1.0, False, feats)
    kept[...] = feats[...]
    cols = feats[...].T.astype(BF16)
    for n, basis in enumerate((basis0, basis1, basis3)):
        if n == 0:
            centres = [tags[pl.ds(2 + k, 1), :] for k in range(3)]
        else:
            ref, at = ((near, 56), (centres3, 0))[n - 1]
            centres = [
                jnp.concatenate(
                    [ref[pl.ds(at + 2 + k, 1), :], ref[pl.ds(at + 10 + k, 1), :]], axis=1
                )
                for k in range(3)
            ]
        basis_of(centres, cols, rows.at[n], squared.at[n], basis)


def edge_kernel(far, jac, tags, out):
    even = (lax.axis_index("cell") & 1) == 0
    at = pl.multiple_of(jnp.where(even, 0, 3 * L), L)
    want = jnp.where(even, 0, 2)
    places = []
    for f in range(NF):
        first, last = tags[pl.ds(11 + f, 1), pl.ds(0, L)], tags[pl.ds(17 + f, 1), pl.ds(L, L)]
        off = jnp.broadcast_to(jnp.where(even, first, last), (8, L)).astype(jnp.int32)
        places.append(iota((8, L), 1) + L + off)
    for t in range(NT):
        sums = [None] * 8
        for f in range(NF):
            got = lanes_of(far[t], places[f] & (L - 1))
            val = jnp.where((places[f] >> 7) == want, got, 0.0)
            gain(sums, jac, f + 1, pl.ds(at, L), val)
        out[t] = fold(sums)


def answer(table, tag, out, own):
    q = lax.axis_index("sec") & 1
    last = iota((8, L), 0) == 7
    total = table[pl.ds(25, 1), :]
    for p in range(1, CHIPS):
        total = total + table[pl.ds(p * ROWS + 25, 1), :]
    total = jnp.broadcast_to(total, (8, L))
    for h in range(2):
        span = pl.ds(h * L, L)
        owner = jnp.broadcast_to(tag[pl.ds(0, 1), span], (8, L)).astype(jnp.int32)
        lane = jnp.broadcast_to(tag[pl.ds(1, 1), span], (8, L)).astype(jnp.int32)
        key = jnp.where((owner & 1) == q, owner >> 1, -1)
        found = [jnp.zeros((8, L), F32) for _ in range(3)]
        for p in range(CHIPS):
            hit = key == p
            for k in range(3):
                values = table[pl.ds(p * ROWS + k * NT, 8), :]
                found[k] = jnp.where(hit, lanes_of(values, lane), found[k])
        for k in range(3):
            extra = jnp.broadcast_to(tag[pl.ds(2 + k, 1), span], (8, L)) if own else 0.0
            out[pl.ds(h * 32 + k * 8, 8), :] = jnp.where(last, extra, found[k])
        out[pl.ds(h * 32 + 24, 8), :] = total


def near_kernel(table, tags, out):
    answer(table, tags, out, True)


def far_kernel(table, other_tags, out):
    answer(table, other_tags, out, False)
    q = lax.axis_index("sec") & 1
    block = (iota((8, L), 1) >> 4) & 1
    for p in range(CHIPS // 2):
        first = table[pl.ds(2 * p * ROWS + 19, 8), :]
        second = table[pl.ds((2 * p + 1) * ROWS + 19, 8), :]
        first = jnp.where(q == 0, pltpu.roll(first, L - 16, 1), first)
        second = jnp.where(q == 0, second, pltpu.roll(second, 16, 1))
        out[pl.ds(64 + p * 8, 8), :] = jnp.where(block == 0, first, second)


def node_sums(source, dense):
    block = iota((8, L), 1) >> 4
    for c in range(4):
        shifted = [source(c * 8 + i) for i in range(8)]
        for g in range(4):
            packed = None
            for i in range(8):
                turn = (16 * i - 32 * g) % L
                moved = pltpu.roll(shifted[i], turn, 1) if turn else shifted[i]
                packed = moved if packed is None else jnp.where(block == i, moved, packed)
            dense[pl.ds(g * 8, 8), pl.ds(c * L, L)] = packed
    tags = dense[pl.ds(29, 1), :].astype(jnp.int32)
    node_hot = jnp.where(iota((L, 512), 0) + 1 == tags, 1.0, 0.0).astype(BF16)
    loads = dot_nt(thirds(dense[...]), node_hot)
    return loads[0:32] + loads[32:64] + loads[64:96]


def own_loads_kernel(table, out, dense):
    q = lax.axis_index("sec") & 1

    def source(p):
        values = table[pl.ds(p * ROWS + 19, 8), :]
        return jnp.where(q == 1, pltpu.roll(values, L - 16, 1), values)

    out[...] = node_sums(source, dense)


def loads_kernel(other, sums, part, out, dense):
    def source(p):
        values = other[pl.ds(64 + p // 2 * 8, 8), :]
        return pltpu.roll(values, L - 16, 1) if p % 2 else values

    loads = node_sums(source, dense) + sums[...]
    for k, t, size, row in RUNS:
        out[k, pl.ds(t, size), :] = part[k, pl.ds(t, size), :] - loads[row : row + size]


def parts_of(values):
    high = values.astype(BF16).astype(F32)
    rest = values - high
    middle = rest.astype(BF16).astype(F32)
    return high, middle, rest - middle


def features(xyz, scale, ones_first, out):
    at = 0
    square = None
    for point in xyz:
        square = point * point if square is None else square + point * point
        p = [scale * part for part in parts_of(point)]
        order = (0, 0, 1, 1, 0, 2) if ones_first else (0, 1, 0, 1, 2, 0)
        for i in order:
            out[pl.ds(at, 1), :] = p[i]
            at += 1
    one = jnp.ones_like(square)
    squares = list(parts_of(square))
    for row in [one] * 3 + squares if ones_first else squares + [one] * 3:
        out[pl.ds(at, 1), :] = row
        at += 1
    out[pl.ds(24, 8), :] = jnp.zeros((8, square.shape[1]), F32)


def basis_of(centres, cols, rows, squared, basis):
    features(centres, -2.0, True, rows)
    squared[...] = jnp.dot(cols, rows[...].astype(BF16), preferred_element_type=F32)
    for c in range(8):
        span = pl.ds(c * 64, 64)
        gap = jnp.maximum(squared[span, :], 1e-30)
        dist = gap * lax.rsqrt(gap)
        fall = jnp.maximum(1.0 - dist, 0.0)
        fall = fall * fall
        value = fall * fall * (4.0 * dist + 1.0)
        high = value.astype(BF16)
        basis[span, pl.ds(0, 256)] = high
        basis[span, pl.ds(256, 256)] = (value - high.astype(F32)).astype(BF16)


def halves(ref):
    return jnp.concatenate([ref[pl.ds(0, 24), :], ref[pl.ds(32, 24), :]], axis=1)


def moved_by(both, basis):
    high = both.astype(BF16).astype(F32)
    upper = jnp.concatenate([high, both - high], axis=0).astype(BF16)
    lower = jnp.concatenate([high, jnp.zeros_like(high)], axis=0).astype(BF16)
    return dot_nt(basis[...], jnp.concatenate([upper, lower], axis=1))


def own_kernel(d0, kept, basis, out, cols):
    cols[...] = kept[...].T
    out[...] = moved_by(halves(d0), basis)


def block_kernel(ref, cols, moved, out, rows, squared, basis):
    both = halves(ref)
    centres = [both[k * 8 + 7 : k * 8 + 8] for k in range(3)]
    basis_of(centres, cols[...].astype(BF16), rows, squared, basis)
    out[...] = moved[...] + moved_by(both, basis)


def third_kernel(d3, basis, moved, out):
    out[...] = moved[...] + moved_by(halves(d3), basis)


def final_kernel(
    d0,
    d1,
    d2,
    d3,
    near_basis,
    moved,
    sens,
    flux,
    edge,
    struct,
    out,
    struct_out,
    phase_out,
):
    struct_out[...] = struct[...]
    even = (lax.axis_index("cell") & 1) == 0
    span = pl.ds(pl.multiple_of(jnp.where(even, 0, 3 * L), L), L)
    total = moved[...] + moved_by(halves(d1), near_basis)
    turned = total.T
    motion = turned[0:24] + turned[24:48]
    for t in range(NT):
        total = flux[t]
        for k in range(3):
            total = total + sens[k] * motion[k * 8 + t : k * 8 + t + 1]
        out[t] = total
        out[t, :, span] = out[t, :, span] + edge[t]
    row = pl.ds(24, 1), pl.ds(0, L)
    total = (d0[row] + d1[row]) + (d2[row] + d3[row])
    total = jnp.where(iota((1, L), 1) >= 96, total, 0.0)
    phase_out[0, 0] = jnp.sum(total)


VM = pl.BlockSpec(memory_space=pltpu.VMEM)
HBM = pl.BlockSpec(memory_space=pltpu.HBM)
SM = pl.BlockSpec(memory_space=pltpu.SMEM)


def kernel(body, name, ins, shapes, outs=None, types=None, scratch=(), size=100000, vmem=32):
    return pl.pallas_call(
        body,
        out_shape=[
            jax.ShapeDtypeStruct(s, t) for s, t in zip(shapes, types or [F32] * len(shapes))
        ],
        in_specs=ins,
        out_specs=outs or [VM] * len(shapes),
        scratch_shapes=list(scratch),
        name=name,
        compiler_params=pltpu.CompilerParams(vmem_limit_bytes=vmem * 1024 * 1024),
        cost_estimate=pl.CostEstimate(flops=1000, bytes_accessed=size, transcendentals=0),
    )


def on_device(
    fluid_delta,
    jacobian,
    face_nbr,
    freq_col,
    grid_sens,
    cell_xyz,
    surf_cell,
    surf_owner,
    surf_node,
    load_proj,
    surf_xyz,
    struct_delta,
    stiffness,
    mass,
    omega,
    freq_delta,
    phase_row,
):
    sections = lax.axis_size("sec")
    columns = lax.axis_size("cell")
    both = sections * columns
    struct = jnp.transpose(struct_delta, (1, 0, 2))
    stiff = jnp.transpose(stiffness, (0, 2, 1, 3))
    jac = jacobian.reshape(NF + 1, 64, 512)
    sens = jnp.transpose(grid_sens, (1, 0, 2))
    owner = surf_owner.reshape(1, 256)
    node = surf_node.reshape(1, 256)
    cell = surf_cell.reshape(1, 256)

    message, tags = kernel(
        prep_kernel,
        "prep",
        [HBM] * 11,
        [(CHIPS * ROWS, L), (56, 256)],
        outs=[HBM, VM],
        scratch=[
            pltpu.VMEM((NT, NV, 512), F32),
            pltpu.VMEM((NT, NV, 512), F32),
            pltpu.VMEM((1, 256), jnp.int32),
            pltpu.VMEM((1, 256), jnp.int32),
            pltpu.VMEM((1, 256), jnp.int32),
            pltpu.VMEM((3, NV, 256), F32),
            pltpu.VMEM((3, NT, L), F32),
            pltpu.VMEM((3, 256), F32),
            pltpu.VMEM((NF, 512), jnp.int32),
            pltpu.VMEM((3, L), F32),
            pltpu.VMEM((3, 512), F32),
            pltpu.VMEM((32, 256), F32),
            pltpu.VMEM((CHIPS * ROWS, L), F32),
            pltpu.SemaphoreType.DMA((11,)),
            pltpu.SemaphoreType.DMA((4,)),
        ],
        vmem=32,
    )(
        *(
            pltpu.with_memory_space_constraint(x, pltpu.HBM)
            for x in (
                fluid_delta,
                phase_row,
                cell,
                owner,
                node,
                load_proj,
                struct,
                surf_xyz,
                face_nbr,
                mass,
                cell_xyz,
            )
        )
    )
    groups = [[2 * i + c for i in range(sections // 2)] for c in range(2)]
    mine = lax.all_to_all(
        message.reshape(CHIPS, 1, ROWS * L), "sec", 0, 0, axis_index_groups=groups, tiled=True
    ).reshape(CHIPS * ROWS, L)
    swap = [(i, i ^ 1) for i in range(sections)]
    other_tags = lax.ppermute(tags, "sec", swap)
    pairs = [[(i, i ^ 1) for i in range(both)], [(i, ((i + 1) ^ 1) - 1) for i in range(1, both - 1)]]
    near_side, far_side, centres = kernel(
        sides_kernel, "sides", [VM] * 2, [(72, L), (NT, NV, L), (16, L)]
    )(fluid_delta, tags)
    centres3 = lax.ppermute(centres, "cell", [(i, i ^ 3) for i in range(columns)])
    near_edge = lax.ppermute(near_side, ("sec", "cell"), pairs[0])
    far_edge = lax.ppermute(far_side, ("sec", "cell"), pairs[1])
    flux, part, kept, *bases = kernel(
        window_kernel,
        "window",
        [VM] * 9,
        [(NT, NV, 512), (3, NT, L), (32, 512)] + [(512, 512)] * 3,
        types=[F32] * 3 + [BF16] * 3,
        scratch=[
            pltpu.VMEM((NF, NT, 8, L), F32),
            pltpu.VMEM((32, 512), F32),
            pltpu.VMEM((3, 32, 256), F32),
            pltpu.VMEM((3, 512, 256), F32),
        ],
        size=4 * 10**6,
    )(
        fluid_delta,
        near_edge,
        centres3,
        jac,
        freq_col,
        stiff,
        tags,
        omega,
        freq_delta,
    )
    mine, flux, far_edge = lax.optimization_barrier((mine, flux, far_edge))
    (far,) = kernel(far_kernel, "far", [VM] * 2, [(192, L)])(mine, other_tags)
    back = lax.ppermute(far, "sec", swap)
    (near,) = kernel(near_kernel, "near", [VM] * 2, [(64, L)])(mine, tags)
    (sums,) = kernel(
        own_loads_kernel, "own_loads", [VM], [(32, L)], scratch=[pltpu.VMEM((32, 512), F32)]
    )(mine)
    back, near, sums = lax.optimization_barrier((back, near, sums))
    disp = near + back[:64]
    d2, d3, d1 = (
        lax.ppermute(disp, "cell", [(i, i ^ k) for i in range(columns)]) for k in (2, 3, 1)
    )
    (struct_out,) = kernel(
        loads_kernel,
        "loads",
        [VM] * 3,
        [(3, NT, L)],
        scratch=[pltpu.VMEM((32, 512), F32)],
        size=2 * 10**6,
    )(back, sums, part)
    moved, cols = kernel(own_kernel, "own", [VM] * 3, [(512, 48), (512, 32)])(
        disp, kept, bases[0]
    )
    (edge,) = kernel(edge_kernel, "edge", [VM] * 3, [(NT, NV, L)])(far_edge, jac, tags)
    struct_out, moved, edge, d2 = lax.optimization_barrier((struct_out, moved, edge, d2))
    (moved,) = kernel(
        block_kernel,
        "block",
        [VM] * 3,
        [(512, 48)],
        scratch=[
            pltpu.VMEM((32, 256), F32),
            pltpu.VMEM((512, 256), F32),
            pltpu.VMEM((512, 512), BF16),
        ],
        size=10**6,
    )(d2, cols, moved)
    (moved,) = kernel(third_kernel, "third", [VM] * 3, [(512, 48)])(d3, bases[2], moved)
    fluid_out, struct_out, phase_out = kernel(
        final_kernel,
        "final",
        [VM] * 10,
        [(NT, NV, 512), (3, NT, L), (1, 1)],
        outs=[VM, VM, SM],
    )(disp, d1, d2, d3, bases[1], moved, sens, flux, edge, struct_out)
    return fluid_out, jnp.transpose(struct_out, (1, 0, 2)), phase_out.reshape(1)


def solution(mesh):
    split = ("sec", "cell")
    return jax.shard_map(
        on_device,
        mesh=mesh,
        in_specs=(
            P(None, None, split),
            P(None, None, None, split),
            P(None, split),
            P(None, None, split),
            P(None, None, split),
            P(None, split),
            P(split),
            P(split, None),
            P(split),
            P(None, None, split),
            P(None, split),
            P(None, None, split),
            P(None, None, None, split),
            P(None, split),
            P(),
            P(),
            P(None, None, split),
        ),
        out_specs=(P(None, None, split), P(None, None, split), P()),
        check_vma=False,
    )
```
